32 devices in a mesh: groups: 2 (over y), expert: 16 (over z, x, core).
Axes of the slice: x: 2, y: 2, z: 4, core: 2. Of those that a mesh axis runs over, the one named last changes fastest.
Arguments:
- tokens: bfloat16 [256, 3584], P(('groups', 'expert')), parts along dimension 0
- moe_gain: float32 [3584], replicated, may hold values from 0.1 to 1.9
- expert_ids: int32 [256, 2], P(('groups', 'expert')), parts along dimension 0, may hold values from 0 to 1, all different within a row; in each aligned block of 8 rows (0 to 7, 8 to 15, ...) at most 8 rows name the same one
- gate_scores: float32 [256, 2], P(('groups', 'expert')), parts along dimension 0, may hold values from 0.05 to 1
- w_gate: bfloat16 [16, 3584, 256], P('expert'), may hold values from -0.09375 to 0.09375
- w_up: bfloat16 [16, 3584, 256], P('expert'), may hold values from -0.09375 to 0.09375
- w_down: bfloat16 [16, 256, 3584], P('expert'), may hold values from -0.125 to 0.125
- final_gain: float32 [3584], replicated, may hold values from 0.1 to 1.9
- teacher_head: bfloat16 [3584, 4096], P(None, 'expert')
- vocab_map: int32 [4096], P('expert'), may hold values from 0 to 255, as said below
- student_logits: bfloat16 [256, 4096], P('groups', 'expert'), parts along dimension 0, may hold values from -16 to 160
- student_head: bfloat16 [2048, 4096], P(None, 'expert'), may hold values from -6 to 6
Outputs:
- divergence: float32 [256], P(('groups', 'expert')), parts along dimension 0
- grad_hidden: float32 [256, 2048], P(('groups', 'expert')), parts along dimension 0
The draws below stay inside these ranges and needn't reach their ends.
There are 2 independent parts, one for each index of `groups`. The reference program is written for one: setup_inputs(seed, part) draws one part's arguments, and reference() takes and returns one part's arrays. A program takes and returns all parts, laid end to end along the dimension named above; an argument that names none is the same for every part. Nothing has to cross between parts.
Inputs may be any that keep to these rules, and one draw needn't show every extreme that they name: `expert_ids`: each row names 2 different experts; the rows of one device name any one expert at most 8 times, a bound that some block reaches. `vocab_map`: each aligned block of 256 entries holds every number of 0 to 255 once.
All inputs are finite; a program needn't handle non-finite values.
Results may differ from the reference program's by a relative error of at most 0.015.
Values may be sent and summed in bfloat16 or wider, within the bound.
No kernel may reach another device: no remote copies, remote signals or barrier semaphores. Data moves between devices by JAX's collectives and lax.ppermute only.
A program may use at most 128 MiB of HBM per device.

```python
import math
import jax
import jax.numpy as jnp
import numpy as np
from jax import lax

D = 3584
FF = 2048
SPLIT = 8
VOC_DEV = 256
DS = 2048
TOK_DEV = 8
FF_DEV = 256
EXPERTS = 2
TOP = 2
CAP = 8
TOKENS = 128
VOCAB = 4096
N_EXPERT = 16


def draw_tokens(key, part):
    base_key, row_key, col_key = jax.random.split(key, 3)
    row_scale = jnp.exp(jax.random.uniform(row_key, (TOKENS, 1), jnp.float32, math.log(0.4), math.log(2.5)))
    col_scale = jnp.exp(jax.random.uniform(col_key, (1, D), jnp.float32, math.log(0.4), math.log(2.5)))
    base = jax.random.normal(base_key, (TOKENS, D), jnp.float32) * row_scale * col_scale
    return base.astype(jnp.bfloat16)


def draw_teacher_head(key, part):
    base_key = jax.random.fold_in(key, 0)
    factor = 3.0 / math.sqrt(D)
    base = jax.random.normal(base_key, (D, VOCAB), jnp.float32) * factor
    return base.astype(jnp.bfloat16)


def permute_block(block_key):
    return jax.random.permutation(block_key, VOC_DEV)


def draw_vocab_map(key, part):
    block_keys = jax.random.split(key, VOCAB // VOC_DEV)
    return jax.vmap(permute_block)(block_keys).reshape(-1).astype(jnp.int32)


def draw_student_logits(key, part):
    base_key = jax.random.fold_in(key, 7)
    base = jnp.clip(jax.random.normal(base_key, (TOKENS, VOCAB), jnp.float32) * 3.0, -15.0, 15.0)
    return base.astype(jnp.bfloat16)


def block_levels(rng, shape, cuts, low, top_value):
    def one(axis_at, blocks):
        heights = jax.random.uniform(jax.random.fold_in(jax.random.fold_in(rng, 6), axis_at), (blocks,), jnp.float32, low / len(cuts), top_value / len(cuts))
        return jnp.repeat(jnp.exp(heights), shape[axis_at] // blocks).reshape((-1,) + (1,) * (len(shape) - axis_at - 1))

    factor_of = one(*cuts[0])
    for cut in cuts[1:]:
        factor_of = factor_of * one(*cut)
    return factor_of


def assign_block(rng, own, number, rows, count, top, most, slope):
    order = jax.random.permutation(rng, count)
    packed, usual = load_shares(count, rows * top, most, slope, True), load_shares(count, rows * top, most, slope, False)
    places = jnp.arange(count)

    def named(sizes, turn):
        used = int((sizes > 0).sum())
        fixed = max(1, used // 4)
        passed = fixed + (places - fixed + turn * (used - fixed)) % max(1, count - fixed)
        return jnp.zeros((count,), jnp.int32).at[order[jnp.where(places < fixed, places, passed)]].set(jnp.asarray(sizes, jnp.int32))

    sizes = jnp.where(number % 4 == 0, named(packed, number // 4), named(usual, number - number // 4 - 1))
    mixed = jax.random.permutation(jax.random.fold_in(own, 3), count)
    source_of, taker = mixed[0:count // 2 * 2:2], mixed[1:count // 2 * 2:2]
    room = jnp.minimum(sizes[source_of] - 1, most - sizes[taker]) // 2
    room = jnp.where((source_of == order[0]) | (taker == order[0]) | (sizes[taker] == 0), 0, jnp.maximum(room, 0))
    passed = jax.random.randint(jax.random.fold_in(own, 4), (count // 2,), 0, 1 << 20) % (room + 1)
    sizes = sizes.at[source_of].add(-passed).at[taker].add(passed)
    labels = jnp.searchsorted(jnp.cumsum(sizes), jnp.arange(rows * top), side="right").astype(jnp.int32)
    listing = labels.reshape(top, rows).T
    listing = listing[jax.random.permutation(jax.random.fold_in(own, 1), rows)]
    turn = jax.random.randint(jax.random.fold_in(own, 2), (rows, 1), 0, top)
    return jnp.take_along_axis(listing, (jnp.arange(top)[None, :] + turn) % top, axis=1)


def load_shares(number_of, total, bound, skew, full):
    weights = [(1 << 20) // math.isqrt(rank ** skew) + 1 for rank in range(1, number_of + 1)]
    largest = bound if full else min(bound, max(-(-total // number_of), total * weights[0] // sum(weights)))
    least = 1 if total - largest >= number_of - 1 else 0
    given, surplus = [largest] + [least] * (number_of - 1), total - largest - least * (number_of - 1)
    while surplus > 0:
        free = [i for i in range(1, number_of) if given[i] < largest] or [i for i in range(1, number_of) if given[i] < bound]
        pool, left = sum([weights[i] for i in free]), surplus
        for i in free:
            extra = min(bound - given[i], max(1, left * weights[i] // pool), surplus)
            given[i] = given[i] + extra
            surplus = surplus - extra
    return np.array(given)


def scatter_about(stream_key, dims, scale, most, cuts=(), held_as=jnp.bfloat16):
    factor_of = block_levels(stream_key, dims, cuts, -0.22, 0.18) if cuts else 1.0
    values = jax.random.normal(stream_key, dims, jnp.float32) * scale * factor_of
    return jnp.minimum(jnp.maximum(values, -most), most).astype(held_as)


def setup_inputs(seed: int = 0, part: int = 0) -> dict:
    seeds = jax.random.split(jax.random.key(seed), 13)
    own_keys = jax.random.split(jax.random.fold_in(seeds[12], part), 13)
    tokens = draw_tokens(jax.random.fold_in(jax.random.fold_in(seeds[12], part), 71), part)
    moe_gain = jnp.clip(1.0 + 0.18 * jax.random.normal(seeds[1], (D,), jnp.float32), 0.1, 1.9)
    expert_ids_keys = jax.random.split(jax.random.fold_in(own_keys[2], 1), TOKENS // TOK_DEV)
    expert_ids_turns = jax.random.permutation(jax.random.fold_in(own_keys[2], 3), TOKENS // TOK_DEV)
    expert_ids = jax.vmap(lambda own, number: assign_block(jax.random.fold_in(own_keys[2], 2), own, number, TOK_DEV, EXPERTS, TOP, CAP, 2))(expert_ids_keys, expert_ids_turns).reshape((TOKENS, TOP))
    gate_scores = jnp.clip(jnp.exp(math.log(1.0) - 2.9957323 * jax.random.uniform(own_keys[3], (TOKENS, TOP), jnp.float32) ** block_levels(own_keys[3], (TOKENS, TOP), ((0, 16),), -0.2, 0.2)), 0.05, 1.0)
    w_gate = scatter_about(seeds[4], (EXPERTS * SPLIT, D, FF_DEV), D ** -0.5, 0.09375, ((0, 16),))
    w_up = scatter_about(seeds[5], (EXPERTS * SPLIT, D, FF_DEV), D ** -0.5, 0.09375, ((0, 16),))
    w_down = scatter_about(seeds[6], (EXPERTS * SPLIT, FF_DEV, D), FF ** -0.5, 0.125, ((0, 16),))
    final_gain = jnp.clip(1.0 + 0.18 * jax.random.normal(seeds[7], (D,), jnp.float32), 0.1, 1.9)
    teacher_head = draw_teacher_head(jax.random.fold_in(seeds[12], 71), part)
    vocab_map = draw_vocab_map(jax.random.fold_in(seeds[12], 71), part)
    student_logits = draw_student_logits(jax.random.fold_in(jax.random.fold_in(seeds[12], part), 71), part)
    student_head = scatter_about(seeds[11], (DS, VOCAB), 1.0, 6.0, ((1, 16),))
    return {"tokens": tokens, "moe_gain": moe_gain, "expert_ids": expert_ids, "gate_scores": gate_scores, "w_gate": w_gate, "w_up": w_up, "w_down": w_down, "final_gain": final_gain, "teacher_head": teacher_head, "vocab_map": vocab_map, "student_logits": student_logits, "student_head": student_head}


EPSILON = 1e-06

def rms_norm(values, gain):
    return values * lax.rsqrt(lax.optimization_barrier(jnp.mean(values * values, axis=-1, keepdims=True)) + EPSILON) * gain

def reference(tokens, moe_gain, expert_ids, gate_scores, w_gate, w_up, w_down, final_gain, teacher_head, vocab_map, student_logits, student_head):
    floats = tokens.astype(jnp.float32)
    normed = rms_norm(floats, moe_gain).astype(jnp.bfloat16)
    weights = gate_scores / lax.optimization_barrier(jnp.sum(gate_scores, axis=1, keepdims=True))
    flat_ids = expert_ids.reshape(-1)
    flat_tok = (jnp.arange(TOKENS * TOP) // TOP).astype(jnp.int32)
    flat_weight = weights.reshape(-1)
    slot_limit = N_EXPERT * CAP

    def add_expert(expert, running):
        matches = flat_ids == expert
        picked = jnp.nonzero(matches, size=slot_limit, fill_value=-1)[0].astype(jnp.int32)
        filled = picked >= 0
        clipped = jnp.maximum(picked, 0)
        targets = flat_tok[clipped]
        inputs = normed[targets].astype(jnp.float32)
        first_piece = (jnp.asarray(expert).astype(jnp.int32) * SPLIT).astype(jnp.int32)
        gate_part = lax.dynamic_slice_in_dim(w_gate, first_piece, SPLIT, 0).astype(jnp.float32)
        up_part = lax.dynamic_slice_in_dim(w_up, first_piece, SPLIT, 0).astype(jnp.float32)
        down_part = lax.dynamic_slice_in_dim(w_down, first_piece, SPLIT, 0).astype(jnp.float32)
        gate_out = jnp.einsum('rd,sdf->rsf', inputs, gate_part)
        up_out = jnp.einsum('rd,sdf->rsf', inputs, up_part)
        activated = (jax.nn.silu(gate_out) * up_out).astype(jnp.bfloat16)
        activated = lax.optimization_barrier(activated).astype(jnp.float32)
        pieces = jnp.einsum('rsf,sfd->rsd', activated, down_part).astype(jnp.bfloat16)
        pieces = lax.optimization_barrier(pieces).astype(jnp.float32)
        summed = lax.optimization_barrier(jnp.sum(pieces, axis=1))
        factor = jnp.where(filled, flat_weight[clipped], jnp.zeros_like(flat_weight[clipped]))
        return running.at[targets].add(summed * factor[:, None])
    moe = lax.fori_loop(0, EXPERTS, add_expert, jnp.zeros((TOKENS, D), jnp.float32))
    hidden = floats + moe
    final_norm = rms_norm(hidden, final_gain).astype(jnp.bfloat16)
    columns = (jnp.arange(VOCAB) // VOC_DEV * VOC_DEV).astype(jnp.int32) + vocab_map.astype(jnp.int32)
    mapped_head = teacher_head[:, columns]
    teacher = jnp.dot(final_norm, mapped_head, preferred_element_type=jnp.float32)
    student = student_logits.astype(jnp.float32)
    teach_max = lax.optimization_barrier(jnp.max(teacher, axis=1))
    teach_exp = jnp.exp(teacher - teach_max[:, None])
    teach_sum = lax.optimization_barrier(jnp.sum(teach_exp, axis=1))
    cross_sum = lax.optimization_barrier(jnp.sum(teach_exp * (teacher - student), axis=1))
    stud_max = lax.optimization_barrier(jnp.max(student, axis=1))
    stud_exp = jnp.exp(student - stud_max[:, None])
    stud_sum = lax.optimization_barrier(jnp.sum(stud_exp, axis=1))
    divergence = cross_sum / teach_sum - teach_max - jnp.log(teach_sum) + stud_max + jnp.log(stud_sum)
    logit_grad = (stud_exp / stud_sum[:, None] - teach_exp / teach_sum[:, None]).astype(jnp.bfloat16)
    grad_hidden = jnp.dot(logit_grad, student_head.T, preferred_element_type=jnp.float32)
    return (divergence, grad_hidden)
```

```python
import functools

import jax
import jax.numpy as jnp
from jax import lax
from jax.experimental import pallas as pl
from jax.experimental.pallas import tpu as pltpu
from jax.sharding import PartitionSpec as P

FF = 2048
EPSILON = 1e-06
F32 = jnp.float32
BF16 = jnp.bfloat16
BLOCK = 128


def radices(devices):
    bits = devices.bit_length() - 1
    x_bits = (bits - 1) // 3
    return 1 << (bits - 1 - x_bits), 1 << x_bits, 2


def dot(a, b):
    return jnp.dot(a, b, preferred_element_type=F32)


def dot_t(a, b):
    return lax.dot_general(a, b, (((1,), (1,)), ((), ())), preferred_element_type=F32)


def lanes(rows):
    return lax.broadcasted_iota(jnp.int32, (rows, BLOCK), 1)


def pack(columns):
    lane = lanes(columns[0].shape[0])
    block = jnp.zeros(lane.shape, F32)
    for j, column in enumerate(columns):
        block = jnp.where((lane % 32 == j) & (lane < 96), column, block)
    return block


def split(block):
    lane = lanes(block.shape[0])
    high = block.astype(BF16)
    rest = block - high.astype(F32)
    middle = rest.astype(BF16)
    low = (rest - middle.astype(F32)).astype(BF16).astype(F32)
    return jnp.where(lane < 32, high.astype(F32), jnp.where(lane < 64, middle.astype(F32), low)).astype(BF16)


def column(block, j, exact):
    lane = lanes(block.shape[0])
    keep = (lane == j) if exact else (lane % 32 == j)
    return jnp.sum(jnp.where(keep, block, 0.0), axis=1, keepdims=True)


def combine(parts, width):
    blocks = [(ref[:, width:].astype(F32), i == 0) for i, ref in enumerate(parts)]
    tops = [column(b, 0, own) for b, own in blocks]
    top = functools.reduce(jnp.maximum, tops)
    scales = [jnp.exp(t - top) for t in tops]
    totals = [sum(column(b, j, own) * s for (b, own), s in zip(blocks, scales)) for j in (1, 2)]
    values = sum(ref[:, :width].astype(F32) * s for ref, s in zip(parts, scales))
    return values, top, totals


def call(body, outs, *args, scratch=(), scalars=0):
    smem = pl.BlockSpec(memory_space=pltpu.SMEM)
    vmem = pl.BlockSpec(memory_space=pltpu.VMEM)
    return pl.pallas_call(
        body,
        out_shape=[jax.ShapeDtypeStruct(s, d) for s, d in outs],
        in_specs=[smem] * scalars + [vmem] * (len(args) - scalars),
        out_specs=[vmem] * len(outs),
        scratch_shapes=list(scratch),
        compiler_params=pltpu.CompilerParams(vmem_limit_bytes=56 * 2**20),
    )(*args)


def normed_rows(values, gain):
    return values * lax.rsqrt(jnp.mean(values * values, axis=-1, keepdims=True) + EPSILON) * gain


def enter_body(tokens, gain, ids, scores, out):
    rows, features = tokens.shape
    out[:, :features] = normed_rows(tokens[...].astype(F32), gain[...]).astype(BF16)
    diagonal = lax.broadcasted_iota(jnp.int32, (rows, rows), 0) == lax.broadcasted_iota(
        jnp.int32, (rows, rows), 1
    )
    lane = lanes(rows) % 64
    block = jnp.zeros(lane.shape, F32)
    total = jnp.zeros((rows, 1), F32)
    for k in range(ids.shape[0]):
        chosen = jnp.where(diagonal, ids[k : k + 1, :].astype(F32), 0.0)
        chosen = jnp.sum(chosen, axis=1, keepdims=True)
        score = jnp.where(diagonal, scores[k : k + 1, :], 0.0)
        score = jnp.sum(score, axis=1, keepdims=True)
        block = block + jnp.where(lane.astype(F32) == chosen, score, 0.0)
        total = total + score
    block = block / total
    high = block.astype(BF16).astype(F32)
    out[:, features:] = jnp.where(lanes(rows) < 64, high, block - high).astype(BF16)


def experts_body(slices, parts, me, *refs):
    inputs, (w_gate, w_up, w_down, send, keep, rows_ref) = refs[:parts], refs[parts:]
    count = inputs[0].shape[0]
    features = w_gate.shape[1]
    for i, ref in enumerate(inputs):
        rows_ref[i * count : (i + 1) * count, :] = ref[...]
    expert = me[0] // slices

    def block(start, size):
        rows = rows_ref[pl.ds(start, size), :features]
        gate = dot(rows, w_gate[0])
        up = dot(rows, w_up[0])
        lane = lanes(size) % 64
        table = rows_ref[pl.ds(start, size), features:].astype(F32)
        weight = jnp.sum(jnp.where(lane == expert, table, 0.0), axis=1, keepdims=True)
        activated = (gate / (1.0 + jnp.exp(-gate)) * up).astype(BF16)
        return activated, weight

    half = parts * count // 2
    if half < BLOCK:
        activated, weight = block(0, 2 * half)
        step = 512
        for at in range(0, features, step):
            out = dot(activated, w_down[0, :, at : at + step]) * weight
            keep[:, at : at + step] = out[:half]
            send[:, at : at + step] = out[half:].astype(BF16)
    else:
        for h, target in enumerate((keep, send)):

            @pl.loop(0, half // BLOCK)
            def _(i):
                start = pl.multiple_of(i * BLOCK, BLOCK)
                activated, weight = block(h * half + start, BLOCK)
                out = dot(activated, w_down[0]) * weight
                target[pl.ds(start, BLOCK), :] = out.astype(target.dtype)


def add_split_body(received, *refs):
    parts, (keep, *sends) = refs[: received + 1], refs[received + 1 :]
    total = sum((ref[...].astype(F32) for ref in parts[1:]), parts[0][...])
    rows = keep.shape[0]
    keep[...] = total[:rows]
    for i, send in enumerate(sends):
        send[...] = total[(i + 1) * rows : (i + 2) * rows].astype(BF16)


def hidden_body(received, *refs):
    parts, (tokens, gain, out) = refs[: received + 1], refs[received + 1 :]
    total = sum((ref[...].astype(F32) for ref in parts[1:]), parts[0][...])
    out[...] = normed_rows(tokens[...].astype(F32) + total, gain[...]).astype(BF16)


def student_body(me, devices, order, vocab_map, logits, head, moved, moved_head, send, keep, scratch):
    entries = logits.shape[1]
    tok_dev = logits.shape[0] // devices
    place = lax.broadcasted_iota(jnp.int32, (entries, entries), 0) == vocab_map[...]
    place = jnp.where(place, 1.0, 0.0).astype(BF16)
    scratch[...] = dot_t(logits[...], place)
    moved_head[...] = dot_t(head[...], place).astype(BF16)
    for slot, offset in enumerate(order):
        source = pl.multiple_of((me[0] ^ offset) * tok_dev, tok_dev)
        moved[slot * tok_dev : (slot + 1) * tok_dev, :] = scratch[pl.ds(source, tok_dev), :]
    half = keep.shape[0]
    width = moved_head.shape[0]
    step = min(half, BLOCK)
    for at in range(0, 2 * half, step):
        student = moved[at : at + step, :]
        top = jnp.max(student, axis=1, keepdims=True)
        exps = jnp.exp(student - top)
        total = jnp.sum(exps, axis=1, keepdims=True)
        emit(at, step, half, width, exps, moved_head, [top, total, jnp.zeros_like(top)], send, keep)


def emit(at, step, half, width, exps, head, columns, send, keep):
    stats = pack(columns)
    values = dot_t(exps.astype(BF16), head[...])
    for start, stop, target in ((0, half, keep), (half, 2 * half, send)):
        low, high = max(at, start), min(at + step, stop)
        if low < high:
            inner, outer = slice(low - at, high - at), slice(low - start, high - start)
            target[outer, :width] = values[inner].astype(target.dtype)
            block = stats[inner]
            target[outer, width:] = block if target is keep else split(block)


def teacher_body(parts, *refs):
    inputs, (head, moved, moved_head, send, keep, rows_ref) = refs[:parts], refs[parts:]
    count = inputs[0].shape[0]
    for i, ref in enumerate(inputs):
        rows_ref[i * count : (i + 1) * count, :] = ref[...]
    half = keep.shape[0]
    width = moved_head.shape[0]
    step = BLOCK
    for at in range(0, 2 * half, step):
        teacher = dot(rows_ref[at : at + step, :], head[...])
        student = moved[at : at + step, :]
        top = jnp.max(teacher, axis=1, keepdims=True)
        exps = jnp.exp(teacher - top)
        total = jnp.sum(exps, axis=1, keepdims=True)
        cross = jnp.sum(exps * (teacher - student), axis=1, keepdims=True)
        emit(at, step, half, width, exps, moved_head, [top, total, cross], send, keep)


def combine_split_body(received, *refs):
    parts, (keep, *sends) = refs[: received + 1], refs[received + 1 :]
    width = keep.shape[1] - BLOCK
    values, top, totals = combine(parts, width)
    stats = pack([top, *totals])
    coded = split(stats)
    rows = keep.shape[0]
    keep[:, :width] = values[:rows]
    keep[:, width:] = stats[:rows]
    for i, send in enumerate(sends):
        inner = slice((i + 1) * rows, (i + 2) * rows)
        send[:, :width] = values[inner].astype(BF16)
        send[:, width:] = coded[inner]


def leave_body(received, *refs):
    teacher, refs = refs[: received + 1], refs[received + 1 :]
    student, (divergence, grad) = refs[: received + 1], refs[received + 1 :]
    width = grad.shape[1]
    teach_values, teach_max, (teach_sum, cross_sum) = combine(teacher, width)
    stud_values, stud_max, (stud_sum, _) = combine(student, width)
    grad[...] = stud_values / stud_sum - teach_values / teach_sum
    value = cross_sum / teach_sum - teach_max - jnp.log(teach_sum) + stud_max + jnp.log(stud_sum)
    rows = grad.shape[0]
    diagonal = lax.broadcasted_iota(jnp.int32, (rows, rows), 0) == lax.broadcasted_iota(
        jnp.int32, (rows, rows), 1
    )
    divergence[...] = jnp.sum(jnp.where(diagonal, value, 0.0), axis=0, keepdims=True)


def per_device(
    tokens,
    moe_gain,
    expert_ids,
    gate_scores,
    w_gate,
    w_up,
    w_down,
    final_gain,
    teacher_head,
    vocab_map,
    student_logits,
    student_head,
):
    devices = lax.axis_size("expert")
    size_z, size_x, _ = radices(devices)
    me = lax.axis_index("expert").astype(jnp.int32).reshape(1)
    tok_dev, features = tokens.shape
    slices = FF // w_gate.shape[2]
    width = student_head.shape[0]
    all_rows = devices * tok_dev
    half, quarter = all_rows // 2, all_rows // (2 * size_x)
    entries = student_head.shape[1]
    order = [
        kz * 2 * size_x + kx * 2 + kc
        for kc in range(2)
        for kx in range(size_x)
        for kz in range(size_z)
    ]

    def swap(values, offset):
        return lax.ppermute(values, "expert", [(i, i ^ offset) for i in range(devices)])

    def gather(rows):
        along_z = [rows] + [swap(rows, kz * 2 * size_x) for kz in range(1, size_z)]
        column = jnp.concatenate(along_z)
        plane = [column] + [swap(column, kx * 2) for kx in range(1, size_x)]
        return plane + [swap(part, 1) for part in plane]

    def scatter(send, keep, body, last):
        cols = keep.shape[1]
        keep, *sends = call(
            functools.partial(body, 1),
            [((quarter, cols), F32)] + [((quarter, cols), BF16)] * (size_x - 1),
            keep,
            swap(send, 1),
        )
        received = [swap(s, 2 * (i + 1)) for i, s in enumerate(sends)]
        keep, *sends = call(
            functools.partial(body, size_x - 1),
            [((tok_dev, cols), F32)] + [((tok_dev, cols), BF16)] * (size_z - 1),
            keep,
            *received,
        )
        received = [swap(s, 2 * size_x * (i + 1)) for i, s in enumerate(sends)]
        return [keep, *received]

    (message,) = call(
        enter_body,
        [((tok_dev, features + BLOCK), BF16)],
        tokens,
        moe_gain.reshape(1, -1),
        expert_ids.T,
        gate_scores.T,
    )

    def student_kernel(me_ref, *refs):
        student_body(me_ref, devices, order, *refs)

    moved, moved_head, stud_send, stud_keep = call(
        student_kernel,
        [
            ((all_rows, entries), F32),
            ((width, entries), BF16),
            ((half, width + BLOCK), BF16),
            ((half, width + BLOCK), F32),
        ],
        me,
        vocab_map.reshape(1, -1),
        student_logits,
        student_head,
        scratch=[pltpu.VMEM((all_rows, entries), F32)],
        scalars=1,
    )
    student = scatter(stud_send, stud_keep, combine_split_body, None)
    arrived = gather(message)
    send, keep = call(
        functools.partial(experts_body, slices, len(arrived)),
        [((half, features), BF16), ((half, features), F32)],
        me,
        *arrived,
        w_gate,
        w_up,
        w_down,
        scratch=[pltpu.VMEM((all_rows, features + BLOCK), BF16)],
        scalars=1,
    )
    summed = scatter(send, keep, add_split_body, None)
    (final_norm,) = call(
        functools.partial(hidden_body, len(summed) - 1),
        [((tok_dev, features), BF16)],
        *summed,
        tokens,
        final_gain.reshape(1, -1),
    )
    arrived = gather(final_norm)
    send, keep = call(
        functools.partial(teacher_body, len(arrived)),
        [((half, width + BLOCK), BF16), ((half, width + BLOCK), F32)],
        *arrived,
        teacher_head,
        moved,
        moved_head,
        scratch=[pltpu.VMEM((all_rows, features), BF16)],
    )
    teacher = scatter(send, keep, combine_split_body, None)
    divergence, grad = call(
        functools.partial(leave_body, len(teacher) - 1),
        [((1, tok_dev), F32), ((tok_dev, width), F32)],
        *teacher,
        *student,
    )
    return divergence.reshape(tok_dev), grad


def solution(mesh):
    placed = (
        P(("groups", "expert"), None),
        P(),
        P(("groups", "expert"), None),
        P(("groups", "expert"), None),
        P("expert", None, None),
        P("expert", None, None),
        P("expert", None, None),
        P(),
        P(None, "expert"),
        P("expert"),
        P("groups", "expert"),
        P(None, "expert"),
    )
    return jax.shard_map(
        per_device,
        mesh=mesh,
        in_specs=placed,
        out_specs=(P(("groups", "expert")), P(("groups", "expert"), None)),
        check_vma=False,
    )
```

```python
import functools

import jax
import jax.numpy as jnp
from jax import lax
from jax.experimental import pallas as pl
from jax.experimental.pallas import tpu as pltpu
from jax.sharding import PartitionSpec as P

FF = 2048
EPSILON = 1e-06
F32 = jnp.float32
BF16 = jnp.bfloat16
BLOCK = 128


def radices(devices):
    bits = devices.bit_length() - 1
    x_bits = (bits - 1) // 3
    return 1 << (bits - 1 - x_bits), 1 << x_bits, 2


def dot(a, b):
    return jnp.dot(a, b, preferred_element_type=F32)


def dot_t(a, b):
    return lax.dot_general(a, b, (((1,), (1,)), ((), ())), preferred_element_type=F32)


def lanes(rows):
    return lax.broadcasted_iota(jnp.int32, (rows, BLOCK), 1)


def pack(columns):
    lane = lanes(columns[0].shape[0])
    block = jnp.zeros(lane.shape, F32)
    for j, column in enumerate(columns):
        block = jnp.where((lane % 32 == j) & (lane < 96), column, block)
    return block


def split(block):
    lane = lanes(block.shape[0])
    high = block.astype(BF16)
    rest = block - high.astype(F32)
    middle = rest.astype(BF16)
    low = (rest - middle.astype(F32)).astype(BF16).astype(F32)
    return jnp.where(lane < 32, high.astype(F32), jnp.where(lane < 64, middle.astype(F32), low)).astype(BF16)


def column(block, j, exact):
    lane = lanes(block.shape[0])
    keep = (lane == j) if exact else (lane % 32 == j)
    return jnp.sum(jnp.where(keep, block, 0.0), axis=1, keepdims=True)


def combine(parts, width):
    blocks = [(ref[:, width:].astype(F32), i == 0) for i, ref in enumerate(parts)]
    tops = [column(b, 0, own) for b, own in blocks]
    top = functools.reduce(jnp.maximum, tops)
    scales = [jnp.exp(t - top) for t in tops]
    totals = [sum(column(b, j, own) * s for (b, own), s in zip(blocks, scales)) for j in (1, 2)]
    values = sum(ref[:, :width].astype(F32) * s for ref, s in zip(parts, scales))
    return values, top, totals


def call(body, outs, *args, scratch=(), scalars=0, after=(), far=0, near=True, near_out=True, limit=16, cost=None):
    smem = pl.BlockSpec(memory_space=pltpu.SMEM)
    vmem = pl.BlockSpec(memory_space=pltpu.VMEM)
    hbm = pl.BlockSpec(memory_space=pltpu.HBM)
    unread = pl.BlockSpec(memory_space=pl.ANY)
    count = len(args)
    middle = count - scalars - far

    def run(*refs):
        body(*refs[:count], *refs[count + len(after) :])

    if near:
        kinds = [None] * scalars + [pltpu.VMEM] * middle + [pltpu.HBM] * far
        args = [a if k is None else pltpu.with_memory_space_constraint(a, k) for a, k in zip(args, kinds)]
    kind = pltpu.VMEM if near and near_out else jax.ShapeDtypeStruct
    return pl.pallas_call(
        run,
        out_shape=[kind(s, d) for s, d in outs],
        in_specs=[smem] * scalars + [vmem] * middle + [hbm] * far + [unread] * len(after),
        out_specs=[vmem] * len(outs),
        scratch_shapes=list(scratch),
        compiler_params=pltpu.CompilerParams(vmem_limit_bytes=(limit if near else 56) * 2**20),
        cost_estimate=cost and pl.CostEstimate(flops=cost[0], bytes_accessed=cost[1], transcendentals=0),
    )(*args, *after)


def fetch(sources, targets, semaphores):
    copies = [
        pltpu.make_async_copy(source, target, semaphores.at[i])
        for i, (source, target) in enumerate(zip(sources, targets))
    ]
    for copy in copies:
        copy.start()
    return copies


def normed_rows(values, gain):
    return values * lax.rsqrt(jnp.mean(values * values, axis=-1, keepdims=True) + EPSILON) * gain[None, :]


def enter_body(tokens_far, gain_far, ids_far, scores_far, out, tokens, gain, ids, scores, semaphores):
    copies = fetch(
        (ids_far, scores_far, tokens_far, gain_far), (ids, scores, tokens, gain), semaphores
    )
    for copy in copies[:2]:
        copy.wait()
    rows, features = tokens.shape
    diagonal = lax.broadcasted_iota(jnp.int32, (rows, rows), 0) == lax.broadcasted_iota(
        jnp.int32, (rows, rows), 1
    )
    lane = lanes(rows) % 64
    block = jnp.zeros(lane.shape, F32)
    total = jnp.zeros((rows, 1), F32)
    for k in range(ids.shape[0]):
        chosen = jnp.where(diagonal, ids[k : k + 1, :].astype(F32), 0.0)
        chosen = jnp.sum(chosen, axis=1, keepdims=True)
        score = jnp.where(diagonal, scores[k : k + 1, :], 0.0)
        score = jnp.sum(score, axis=1, keepdims=True)
        block = block + jnp.where(lane.astype(F32) == chosen, score, 0.0)
        total = total + score
    block = block / total
    high = block.astype(BF16).astype(F32)
    out[:, features:] = jnp.where(lanes(rows) < 64, high, block - high).astype(BF16)
    for copy in copies[2:]:
        copy.wait()
    out[:, :features] = normed_rows(tokens[...].astype(F32), gain[...]).astype(BF16)


def paired(out):
    return [slice(at, at + 16) for at in range(0, out.shape[0], 16)]


def join_body(*refs):
    *parts, out = refs
    for rows, pair in zip(paired(out), zip(*[iter(parts)] * 2)):
        out[rows, :] = jnp.concatenate([p[...].astype(F32) for p in pair]).astype(BF16)


def experts_body(slices, parts, me, *refs):
    inputs, (w_gate, w_up, w_down, keep, send, rows_ref) = refs[:parts], refs[parts:]
    count = inputs[0].shape[0]
    features = w_gate.shape[1]
    for i, ref in enumerate(inputs):
        rows_ref[i * count : (i + 1) * count, :] = ref[:, : rows_ref.shape[1]]
    expert = me[0] // slices

    def block(start, size):
        rows = rows_ref[pl.ds(start, size), :features]
        gate = dot(rows, w_gate[0])
        up = dot(rows, w_up[0])
        lane = lanes(size) % 64
        table = rows_ref[pl.ds(start, size), features:].astype(F32)
        weight = jnp.sum(jnp.where(lane == expert, table, 0.0), axis=1, keepdims=True)
        activated = (gate / (1.0 + jnp.exp(-gate)) * up).astype(BF16)
        return activated, weight

    half = parts * count // 2
    if half < BLOCK:
        activated, weight = block(0, 2 * half)
        step = 512
        for at in range(0, features, step):
            out = dot(activated, w_down[0, :, at : at + step]) * weight
            keep[:, at : at + step] = out[:half]
            send[:, at : at + step] = out[half:].astype(BF16)
    else:
        for h, target in enumerate((keep, send)):

            @pl.loop(0, half // BLOCK)
            def _(i):
                start = pl.multiple_of(i * BLOCK, BLOCK)
                activated, weight = block(h * half + start, BLOCK)
                out = dot(activated, w_down[0]) * weight
                target[pl.ds(start, BLOCK), :] = out.astype(target.dtype)


def add_split_body(received, *refs):
    parts, (keep, *sends) = refs[: received + 1], refs[received + 1 :]
    total = sum((ref[...].astype(F32) for ref in parts[1:]), parts[0][...])
    rows = keep.shape[0]
    keep[...] = total[:rows]
    for i, send in enumerate(sends):
        at = (len(sends) - i) * rows
        send[...] = total[at : at + rows].astype(BF16)


def hidden_body(received, *refs):
    parts, (tokens, gain, out) = refs[: received + 1], refs[received + 1 :]
    total = sum((ref[...].astype(F32) for ref in parts[1:]), parts[0][...])
    out[...] = normed_rows(tokens[...].astype(F32) + total, gain[...]).astype(BF16)


def student_body(devices, order, prefetched, me, vocab_far, logits_far, head_far, *refs):
    sources, (moved, moved_head, keep, send, *refs) = refs[:prefetched], refs[prefetched:]
    targets, (vocab_map, logits, head, scratch, semaphores) = refs[:prefetched], refs[prefetched:]
    copies = fetch(
        (vocab_far, logits_far, head_far, *sources), (vocab_map, logits, head, *targets), semaphores
    )
    for copy in copies[:3]:
        copy.wait()
    entries = logits.shape[1]
    tok_dev = logits.shape[0] // devices
    place = lax.broadcasted_iota(jnp.int32, (entries, entries), 0) == vocab_map[...][None, :]
    place = jnp.where(place, 1.0, 0.0).astype(BF16)
    scratch[...] = dot_t(logits[...], place)
    moved_head[...] = dot_t(head[...], place).astype(BF16)
    for slot, offset in enumerate(order):
        source = pl.multiple_of((me[0] ^ offset) * tok_dev, tok_dev)
        moved[slot * tok_dev : (slot + 1) * tok_dev, :] = scratch[pl.ds(source, tok_dev), :]
    half = keep.shape[0]
    width = moved_head.shape[0]
    step = min(half, BLOCK)
    for at in range(0, 2 * half, step):
        student = moved[at : at + step, :]
        top = jnp.max(student, axis=1, keepdims=True)
        exps = jnp.exp(student - top)
        total = jnp.sum(exps, axis=1, keepdims=True)
        emit(at, step, half, width, exps, moved_head, [top, total, jnp.zeros_like(top)], send, keep)
    for copy in copies[3:]:
        copy.wait()


def emit(at, step, half, width, exps, head, columns, send, keep):
    stats = pack(columns)
    values = dot_t(exps.astype(BF16), head[...])
    for start, stop, target in ((0, half, keep), (half, 2 * half, send)):
        low, high = max(at, start), min(at + step, stop)
        if low < high:
            inner, outer = slice(low - at, high - at), slice(low - start, high - start)
            target[outer, :width] = values[inner].astype(target.dtype)
            block = stats[inner]
            target[outer, width:] = block if target is keep else split(block)


def teacher_body(parts, *refs):
    inputs, (head, moved, moved_head, keep, send, rows_ref) = refs[:parts], refs[parts:]
    count = inputs[0].shape[0]
    for i, ref in enumerate(inputs):
        rows_ref[i * count : (i + 1) * count, :] = ref[...]
    half = keep.shape[0]
    width = moved_head.shape[0]
    step = BLOCK
    for at in range(0, 2 * half, step):
        teacher = dot(rows_ref[at : at + step, :], head[...])
        student = moved[at : at + step, :]
        top = jnp.max(teacher, axis=1, keepdims=True)
        exps = jnp.exp(teacher - top)
        total = jnp.sum(exps, axis=1, keepdims=True)
        cross = jnp.sum(exps * (teacher - student), axis=1, keepdims=True)
        emit(at, step, half, width, exps, moved_head, [top, total, cross], send, keep)


def combine_split_body(received, *refs):
    parts, (keep, *sends) = refs[: received + 1], refs[received + 1 :]
    width = keep.shape[1] - BLOCK
    values, top, totals = combine(parts, width)
    stats = pack([top, *totals])
    coded = split(stats)
    rows = keep.shape[0]
    keep[:, :width] = values[:rows]
    keep[:, width:] = stats[:rows]
    for i, send in enumerate(sends):
        at = (len(sends) - i) * rows
        inner = slice(at, at + rows)
        send[:, :width] = values[inner].astype(BF16)
        send[:, width:] = coded[inner]


def add_both_body(size_x, size_z, *refs):
    moe, refs = refs[:size_x], refs[size_x:]
    student, refs = refs[:2], refs[2:]
    add_split_body(size_x - 1, *moe, *refs[:size_z])
    combine_split_body(1, *student, *refs[size_z:])


def pass_body(*refs):
    for source, target in zip(refs[: len(refs) // 2], refs[len(refs) // 2 :]):
        target[...] = source[...]


def join_both_body(size_z, size_x, *refs):
    parts, refs = refs[:size_z], refs[size_z:]
    student, (out, *outs) = refs[:size_x], refs[size_x:]
    join_body(*parts, out)
    combine_split_body(size_x - 1, *student, *outs)


def leave_body(received, *refs):
    teacher, refs = refs[: received + 1], refs[received + 1 :]
    student, (divergence, grad) = refs[: received + 1], refs[received + 1 :]
    width = grad.shape[1]
    teach_values, teach_max, (teach_sum, cross_sum) = combine(teacher, width)
    stud_values, stud_max, (stud_sum, _) = combine(student, width)
    grad[...] = stud_values / stud_sum - teach_values / teach_sum
    value = cross_sum / teach_sum - teach_max - jnp.log(teach_sum) + stud_max + jnp.log(stud_sum)
    rows = grad.shape[0]
    diagonal = lax.broadcasted_iota(jnp.int32, (rows, rows), 0) == lax.broadcasted_iota(
        jnp.int32, (rows, rows), 1
    )
    divergence[...] = jnp.sum(jnp.where(diagonal, value, 0.0), axis=0, keepdims=True)


def take(outs):
    return outs[0], outs[1:]


def per_device(
    tokens,
    moe_gain,
    expert_ids,
    gate_scores,
    w_gate,
    w_up,
    w_down,
    final_gain,
    teacher_head,
    vocab_map,
    student_logits,
    student_head,
):
    devices = lax.axis_size("expert")
    size_z, size_x, _ = radices(devices)
    me = lax.axis_index("expert").astype(jnp.int32).reshape(1)
    tok_dev, features = tokens.shape
    slices = FF // w_gate.shape[2]
    width = student_head.shape[0]
    all_rows = devices * tok_dev
    half, quarter = all_rows // 2, all_rows // (2 * size_x)
    entries = student_head.shape[1]
    order = [
        kz * 2 * size_x + kx * 2 + kc
        for kc in range(2)
        for kx in range(size_x)
        for kz in range(size_z)
    ]

    near = all_rows <= BLOCK
    run = functools.partial(call, near=near)

    def swap(values, offset):
        return lax.ppermute(values, "expert", [(i, i ^ offset) for i in range(devices)])

    def along_z(rows):
        return [rows] + [swap(rows, kz * 2 * size_x) for kz in range(1, size_z)]

    def along_x(column):
        return [column] + [swap(column, kx * 2) for kx in range(1, size_x)]

    def over_cores(plane):
        return plane + [swap(part, 1) for part in plane]

    def add_cores(keep, send, body, after=()):
        outs = [((quarter, keep.shape[1]), d) for d in [F32] + [BF16] * (size_x - 1)]
        return run(functools.partial(body, 1), outs, keep, swap(send, 1), after=after)

    def add_x(keep, sends, body, after=()):
        outs = [((tok_dev, keep.shape[1]), d) for d in [F32] + [BF16] * (size_z - 1)]
        return run(functools.partial(body, size_x - 1), outs, keep, *sends, after=after)

    def along(sends):
        return [swap(s, 2 * (size_x - 1 - i)) for i, s in enumerate(sends)]

    def from_z(keep, sends):
        return [keep] + [swap(s, 2 * size_x * (size_z - 1 - i)) for i, s in enumerate(sends)]

    (message,) = run(
        enter_body,
        [((tok_dev, features + BLOCK), BF16)],
        tokens,
        moe_gain,
        expert_ids.T,
        gate_scores.T,
        scratch=[
            pltpu.VMEM((tok_dev, features), BF16),
            pltpu.VMEM((features,), F32),
            pltpu.VMEM(expert_ids.T.shape, jnp.int32),
            pltpu.VMEM(expert_ids.T.shape, F32),
            pltpu.SemaphoreType.DMA((4,)),
        ],
        far=4,
    )
    (column_rows,) = run(join_body, [((quarter, features + BLOCK), BF16)], *along_z(message))
    plane = along_x(column_rows)
    prefetched = [w_gate, w_up, w_down, teacher_head, tokens, final_gain]
    fetched = prefetched if near else []
    moved, moved_head, stud_keep, stud_send, *ready = run(
        functools.partial(student_body, devices, order, len(fetched)),
        [
            ((all_rows, entries), F32),
            ((width, entries), BF16),
            ((half, width + BLOCK), F32),
            ((half, width + BLOCK), BF16),
            *[(a.shape, a.dtype) for a in fetched],
        ],
        me,
        vocab_map,
        student_logits,
        student_head,
        *fetched,
        scratch=[
            pltpu.VMEM((entries,), jnp.int32),
            pltpu.VMEM((all_rows, entries), BF16),
            pltpu.VMEM((width, entries), BF16),
            pltpu.VMEM((all_rows, entries), F32),
            pltpu.SemaphoreType.DMA((3 + len(fetched),)),
        ],
        scalars=1,
        far=3 + len(fetched),
        cost=(2 * entries * width * (all_rows + entries), 2 * sum(a.size for a in prefetched)),
        after=[column_rows],
    )
    w_gate, w_up, w_down, teacher_head, tokens, final_gain = ready if near else prefetched
    crossed = run(
        pass_body, [(p.shape, p.dtype) for p in plane[1:]], *plane[1:], after=[stud_keep]
    )
    arrived = over_cores([column_rows, *crossed])
    keep, send = run(
        functools.partial(experts_body, slices, len(arrived)),
        [((half, features), F32), ((half, features), BF16)],
        me,
        *arrived,
        w_gate,
        w_up,
        w_down,
        scratch=[pltpu.VMEM((all_rows, features + BLOCK), BF16)],
        scalars=1,
    )
    keep, *sends = add_cores(keep, send, add_split_body)
    outs = run(
        functools.partial(add_both_body, size_x, size_z),
        [((tok_dev, features), d) for d in [F32] + [BF16] * (size_z - 1)]
        + [((quarter, width + BLOCK), d) for d in [F32] + [BF16] * (size_x - 1)],
        keep,
        *along(sends),
        stud_keep,
        swap(stud_send, 1),
    )
    summed = from_z(*take(outs[:size_z]))
    stud_keep, *stud_sends = outs[size_z:]
    (final_norm,) = run(
        functools.partial(hidden_body, len(summed) - 1),
        [((tok_dev, features), BF16)],
        *summed,
        tokens,
        final_gain,
    )
    column_rows, *outs = run(
        functools.partial(join_both_body, size_z, size_x),
        [((quarter, features), BF16)]
        + [((tok_dev, width + BLOCK), d) for d in [F32] + [BF16] * (size_z - 1)],
        *along_z(final_norm),
        stud_keep,
        *along(stud_sends),
    )
    student = from_z(*take(outs))
    arrived = over_cores(along_x(column_rows))
    keep, send = run(
        functools.partial(teacher_body, len(arrived)),
        [((half, width + BLOCK), F32), ((half, width + BLOCK), BF16)],
        *arrived,
        teacher_head,
        moved,
        moved_head,
        scratch=[pltpu.VMEM((all_rows, features), BF16)],
    )
    keep, *sends = add_cores(keep, send, combine_split_body)
    teacher = from_z(*take(add_x(keep, along(sends), combine_split_body)))
    divergence, grad = run(
        functools.partial(leave_body, len(teacher) - 1),
        [((1, tok_dev), F32), ((tok_dev, width), F32)],
        *teacher,
        *student,
        near_out=False,
    )
    return divergence.reshape(tok_dev), grad


def solution(mesh):
    placed = (
        P(("groups", "expert")),
        P(),
        P(("groups", "expert")),
        P(("groups", "expert")),
        P("expert", None),
        P("expert", None),
        P("expert", None),
        P(),
        P(None, "expert"),
        P("expert"),
        P("groups", "expert"),
        P(None, "expert"),
    )
    return jax.shard_map(
        per_device,
        mesh=mesh,
        in_specs=placed,
        out_specs=(P(("groups", "expert")), P(("groups", "expert"))),
        check_vma=False,
    )
```

```python
import functools

import jax
import jax.numpy as jnp
from jax import lax
from jax.experimental import pallas as pl
from jax.experimental.pallas import tpu as pltpu
from jax.sharding import PartitionSpec as P

FF = 2048
EPSILON = 1e-06
F32 = jnp.float32
BF16 = jnp.bfloat16
BLOCK = 128


def radices(devices):
    bits = devices.bit_length() - 1
    x_bits = (bits - 1) // 3
    return 1 << (bits - 1 - x_bits), 1 << x_bits, 2


def dot(a, b):
    return jnp.dot(a, b, preferred_element_type=F32)


def dot_t(a, b):
    return lax.dot_general(a, b, (((1,), (1,)), ((), ())), preferred_element_type=F32)


def lanes(rows):
    return lax.broadcasted_iota(jnp.int32, (rows, BLOCK), 1)


def pack(columns):
    lane = lanes(columns[0].shape[0])
    block = jnp.zeros(lane.shape, F32)
    for j, column in enumerate(columns):
        block = jnp.where((lane % 32 == j) & (lane < 96), column, block)
    return block


def split(block):
    lane = lanes(block.shape[0])
    high = block.astype(BF16)
    rest = block - high.astype(F32)
    middle = rest.astype(BF16)
    low = (rest - middle.astype(F32)).astype(BF16).astype(F32)
    return jnp.where(lane < 32, high.astype(F32), jnp.where(lane < 64, middle.astype(F32), low)).astype(BF16)


def column(block, j, exact):
    lane = lanes(block.shape[0])
    keep = (lane == j) if exact else (lane % 32 == j)
    return jnp.sum(jnp.where(keep, block, 0.0), axis=1, keepdims=True)


def combine(parts, width):
    blocks = [(ref[:, width:].astype(F32), i == 0) for i, ref in enumerate(parts)]
    tops = [column(b, 0, own) for b, own in blocks]
    top = functools.reduce(jnp.maximum, tops)
    scales = [jnp.exp(t - top) for t in tops]
    totals = [sum(column(b, j, own) * s for (b, own), s in zip(blocks, scales)) for j in (1, 2)]
    values = sum(ref[:, :width].astype(F32) * s for ref, s in zip(parts, scales))
    return values, top, totals


def call(body, outs, *args, scratch=(), scalars=0, after=(), far=0, near=True, near_out=True, limit=12, cost=None):
    smem = pl.BlockSpec(memory_space=pltpu.SMEM)
    vmem = pl.BlockSpec(memory_space=pltpu.VMEM)
    hbm = pl.BlockSpec(memory_space=pltpu.HBM)
    unread = pl.BlockSpec(memory_space=pl.ANY)
    count = len(args)
    middle = count - scalars - far

    def run(*refs):
        body(*refs[:count], *refs[count + len(after) :])

    if near:
        kinds = [None] * scalars + [pltpu.VMEM] * middle + [pltpu.HBM] * far
        args = [a if k is None else pltpu.with_memory_space_constraint(a, k) for a, k in zip(args, kinds)]
    kind = pltpu.VMEM if near and near_out else jax.ShapeDtypeStruct
    return pl.pallas_call(
        run,
        out_shape=[kind(s, d) for s, d in outs],
        in_specs=[smem] * scalars + [vmem] * middle + [hbm] * far + [unread] * len(after),
        out_specs=[vmem] * len(outs),
        scratch_shapes=list(scratch),
        compiler_params=pltpu.CompilerParams(vmem_limit_bytes=(limit if near else 56) * 2**20),
        cost_estimate=cost and pl.CostEstimate(flops=cost[0], bytes_accessed=cost[1], transcendentals=0),
    )(*args, *after)


def fetch(sources, targets, semaphores):
    copies = [
        pltpu.make_async_copy(source, target, semaphores.at[i])
        for i, (source, target) in enumerate(zip(sources, targets))
    ]
    for copy in copies:
        copy.start()
    return copies


def fetch_body(source, target, semaphores):
    for copy in fetch((source,), (target,), semaphores):
        copy.wait()


def normed_rows(values, gain):
    return values * lax.rsqrt(jnp.mean(values * values, axis=-1, keepdims=True) + EPSILON) * gain[None, :]


def enter_body(tokens_far, gain_far, ids_far, scores_far, logits_far, map_far, *refs):
    *outs, entries, tokens, gain, ids, scores, vocab_map, semaphores = refs
    count = logits_far.shape[0]
    copies = fetch(
        (ids_far, scores_far, tokens_far, gain_far, map_far, logits_far),
        (ids, scores, tokens, gain, vocab_map, entries.at[:count]),
        semaphores,
    )
    for copy in copies[:2]:
        copy.wait()
    rows, features = tokens.shape
    diagonal = lax.broadcasted_iota(jnp.int32, (rows, rows), 0) == lax.broadcasted_iota(
        jnp.int32, (rows, rows), 1
    )
    lane = lanes(rows) % 64
    block = jnp.zeros(lane.shape, F32)
    total = jnp.zeros((rows, 1), F32)
    for k in range(ids.shape[0]):
        chosen = jnp.where(diagonal, ids[k : k + 1, :].astype(F32), 0.0)
        chosen = jnp.sum(chosen, axis=1, keepdims=True)
        score = jnp.where(diagonal, scores[k : k + 1, :], 0.0)
        score = jnp.sum(score, axis=1, keepdims=True)
        block = block + jnp.where(lane.astype(F32) == chosen, score, 0.0)
        total = total + score
    block = block / total
    high = block.astype(BF16).astype(F32)
    table = jnp.where(lanes(rows) < 64, high, block - high).astype(BF16)
    for copy in copies[2:]:
        copy.wait()
    normed = normed_rows(tokens[...].astype(F32), gain[...]).astype(BF16)
    for out in outs:
        out[:, :features] = normed
        out[:, features:] = table
    places = vocab_map[...].astype(F32)[None, :]
    entries[count:, :] = jnp.broadcast_to(places, (16, places.shape[1])).astype(BF16)


def paired(out):
    return [slice(at, at + 16) for at in range(0, out.shape[0], 16)]


def join_body(*refs):
    *parts, out = refs
    for rows, pair in zip(paired(out), zip(*[iter(reversed(parts))] * 2)):
        out[rows, :] = jnp.concatenate([p[...].astype(F32) for p in pair]).astype(BF16)


def experts_body(slices, parts, me, *refs):
    inputs, (w_gate, w_up, w_down, keep, send, rows_ref) = refs[:parts], refs[parts:]
    count = inputs[0].shape[0]
    features = w_gate.shape[1]
    for i, ref in enumerate(inputs):
        rows_ref[i * count : (i + 1) * count, :] = ref[:, : rows_ref.shape[1]]
    expert = me[0] // slices

    def block(start, size):
        rows = rows_ref[pl.ds(start, size), :features]
        gate = dot(rows, w_gate[0])
        up = dot(rows, w_up[0])
        lane = lanes(size) % 64
        table = rows_ref[pl.ds(start, size), features:].astype(F32)
        weight = jnp.sum(jnp.where(lane == expert, table, 0.0), axis=1, keepdims=True)
        activated = (gate / (1.0 + jnp.exp(-gate)) * up).astype(BF16)
        return activated, weight

    half = parts * count // 2
    if half < BLOCK:
        activated, weight = block(0, 2 * half)
        step = 512
        for at in range(0, features, step):
            out = dot(activated, w_down[0, :, at : at + step]) * weight
            keep[:, at : at + step] = out[:half]
            send[:, at : at + step] = out[half:].astype(BF16)
    else:
        for h, target in enumerate((keep, send)):

            @pl.loop(0, half // BLOCK)
            def _(i):
                start = pl.multiple_of(i * BLOCK, BLOCK)
                activated, weight = block(h * half + start, BLOCK)
                out = dot(activated, w_down[0]) * weight
                target[pl.ds(start, BLOCK), :] = out.astype(target.dtype)


def add_split_body(received, *refs):
    parts, (keep, *sends) = refs[: received + 1], refs[received + 1 :]
    total = sum((ref[...].astype(F32) for ref in parts[1:]), parts[0][...])
    rows = keep.shape[0]
    keep[...] = total[:rows]
    for i, send in enumerate(sends):
        at = (len(sends) - i) * rows
        send[...] = total[at : at + rows].astype(BF16)


def hidden_body(received, passing, *refs):
    parts, (tokens, gain, *refs) = refs[: received + 1], refs[received + 1 :]
    passed, outs = refs[:passing], refs[passing:]
    total = sum((ref[...].astype(F32) for ref in parts[1:]), parts[0][...])
    normed = normed_rows(tokens[...].astype(F32) + total, gain[...]).astype(BF16)
    for out in outs[: len(outs) - passing]:
        out[...] = normed
    for source, target in zip(passed, outs[len(outs) - passing :]):
        target[...] = source[...]


def student_body(devices, order, prefetched, me, ours, theirs, their_head, head_far, *refs):
    sources, (moved, moved_head, *refs) = refs[:prefetched], refs[prefetched:]
    outs = len(refs) - prefetched - 3
    parts, targets, (head, scratch, semaphores) = (
        refs[:outs],
        refs[outs : outs + prefetched],
        refs[outs + prefetched :],
    )
    copies = fetch((head_far, *sources), (head, *targets), semaphores)
    copies[0].wait()
    count = scratch.shape[0]
    entries = head.shape[1]
    tok_dev = count // devices
    for i, (rows, weights) in enumerate(((ours, head), (theirs, their_head))):
        cols = slice(i * entries, (i + 1) * entries)
        index = lax.broadcasted_iota(jnp.int32, (entries, entries), 0).astype(F32)
        place = index == rows[count:, :].astype(F32)[:1, :]
        place = jnp.where(place, 1.0, 0.0).astype(BF16)
        scratch[:, cols] = dot_t(rows[:count, :], place)
        moved_head[:, cols] = dot_t(weights[...], place).astype(BF16)
    for slot, offset in enumerate(order):
        source = pl.multiple_of((me[0] ^ offset) * tok_dev, tok_dev)
        moved[slot * tok_dev : (slot + 1) * tok_dev, :] = scratch[pl.ds(source, tok_dev), :]
    step = min(moved.shape[0], BLOCK)
    for at in range(0, moved.shape[0], step):
        student = moved[at : at + step, :]
        top = jnp.max(student, axis=1, keepdims=True)
        exps = jnp.exp(student - top)
        total = jnp.sum(exps, axis=1, keepdims=True)
        emit(at, step, exps, moved_head, [top, total, jnp.zeros_like(top)], parts)
    for copy in copies[1:]:
        copy.wait()


def emit(at, step, exps, head, columns, targets):
    stats = pack(columns)
    values = dot_t(exps.astype(BF16), head[...])
    width = head.shape[0]
    for i, target in enumerate(targets):
        rows = target.shape[0]
        low, high = max(at, i * rows), min(at + step, (i + 1) * rows)
        if low < high:
            inner, outer = slice(low - at, high - at), slice(low - i * rows, high - i * rows)
            target[outer, :width] = values[inner].astype(target.dtype)
            target[outer, width:] = stats[inner] if i == 0 else split(stats[inner])


def teacher_body(parts, *refs):
    inputs, (head, their_head, moved, moved_head, *targets, rows_ref) = refs[:parts], refs[parts:]
    count = inputs[0].shape[0]
    for i, ref in enumerate(inputs):
        rows_ref[i * count : (i + 1) * count, :] = ref[...]
    step = min(parts * count, BLOCK)
    for at in range(0, parts * count, step):
        rows = rows_ref[at : at + step, :]
        teacher = jnp.concatenate([dot(rows, head[...]), dot(rows, their_head[...])], axis=1)
        student = moved[at : at + step, :]
        top = jnp.max(teacher, axis=1, keepdims=True)
        exps = jnp.exp(teacher - top)
        total = jnp.sum(exps, axis=1, keepdims=True)
        cross = jnp.sum(exps * (teacher - student), axis=1, keepdims=True)
        emit(at, step, exps, moved_head, [top, total, cross], targets)


def combine_split_body(received, *refs):
    parts, (keep, *sends) = refs[: received + 1], refs[received + 1 :]
    width = keep.shape[1] - BLOCK
    values, top, totals = combine(parts, width)
    stats = pack([top, *totals])
    coded = split(stats)
    rows = keep.shape[0]
    keep[:, :width] = values[:rows]
    keep[:, width:] = stats[:rows]
    for i, send in enumerate(sends):
        at = (len(sends) - i) * rows
        inner = slice(at, at + rows)
        send[:, :width] = values[inner].astype(BF16)
        send[:, width:] = coded[inner]


def pass_body(*refs):
    for source, target in zip(refs[: len(refs) // 2], refs[len(refs) // 2 :]):
        target[...] = source[...]


def join_both_body(size_z, size_x, *refs):
    parts, refs = refs[:size_z], refs[size_z:]
    student, (out, *outs) = refs[:size_x], refs[size_x:]
    join_body(*parts, out)
    combine_split_body(size_x - 1, *student, *outs)


def leave_body(received, *refs):
    teacher, refs = refs[: received + 1], refs[received + 1 :]
    student, (divergence, grad) = refs[: received + 1], refs[received + 1 :]
    width = grad.shape[1]
    teach_values, teach_max, (teach_sum, cross_sum) = combine(teacher, width)
    stud_values, stud_max, (stud_sum, _) = combine(student, width)
    grad[...] = stud_values / stud_sum - teach_values / teach_sum
    value = cross_sum / teach_sum - teach_max - jnp.log(teach_sum) + stud_max + jnp.log(stud_sum)
    rows = grad.shape[0]
    diagonal = lax.broadcasted_iota(jnp.int32, (rows, rows), 0) == lax.broadcasted_iota(
        jnp.int32, (rows, rows), 1
    )
    divergence[...] = jnp.sum(jnp.where(diagonal, value, 0.0), axis=0, keepdims=True)


def take(outs):
    return outs[0], outs[1:]


def per_device(
    tokens,
    moe_gain,
    expert_ids,
    gate_scores,
    w_gate,
    w_up,
    w_down,
    final_gain,
    teacher_head,
    vocab_map,
    student_logits,
    student_head,
):
    devices = lax.axis_size("expert")
    size_z, size_x, _ = radices(devices)
    me = lax.axis_index("expert").astype(jnp.int32).reshape(1)
    tok_dev, features = tokens.shape
    slices = FF // w_gate.shape[2]
    width = student_head.shape[0]
    all_rows = devices * tok_dev
    half, quarter = all_rows // 2, all_rows // (2 * size_x)
    entries = student_head.shape[1]
    order = [kz * 2 * size_x + kx * 2 for kx in range(size_x) for kz in range(size_z)]
    near = all_rows <= BLOCK
    run = functools.partial(call, near=near)

    def swap(values, offset):
        return lax.ppermute(values, "expert", [(i, i ^ offset) for i in range(devices)])

    def along_z(rows):
        far = [swap(a, kz * 2 * size_x) for kz, a in reversed(list(enumerate(rows))[1:])]
        return [*far, rows[0]]

    def along_x(column):
        return [column] + [swap(column, kx * 2) for kx in range(1, size_x)]

    def over_cores(plane):
        return plane + [swap(part, 1) for part in plane]

    def add_cores(keep, send, body, after=()):
        outs = [((quarter, keep.shape[1]), d) for d in [F32] + [BF16] * (size_x - 1)]
        return run(functools.partial(body, 1), outs, keep, swap(send, 1), after=after)

    def add_x(keep, sends, body, after=()):
        outs = [((tok_dev, keep.shape[1]), d) for d in [F32] + [BF16] * (size_z - 1)]
        return run(functools.partial(body, size_x - 1), outs, keep, *sends, after=after)

    def along(sends):
        return [swap(s, 2 * (size_x - 1 - i)) for i, s in enumerate(sends)]

    def from_z(keep, sends):
        return [keep] + [swap(s, 2 * size_x * (size_z - 1 - i)) for i, s in enumerate(sends)]

    *messages, ours = run(
        enter_body,
        [((tok_dev, features + BLOCK), BF16)] * size_z + [((all_rows + 16, entries), BF16)],
        tokens,
        moe_gain,
        expert_ids.T,
        gate_scores.T,
        student_logits,
        vocab_map,
        scratch=[
            pltpu.VMEM((tok_dev, features), BF16),
            pltpu.VMEM((features,), F32),
            pltpu.VMEM(expert_ids.T.shape, jnp.int32),
            pltpu.VMEM(expert_ids.T.shape, F32),
            pltpu.VMEM((entries,), jnp.int32),
            pltpu.SemaphoreType.DMA((6,)),
        ],
        far=6,
    )
    (column_rows,) = run(join_body, [((quarter, features + BLOCK), BF16)], *along_z(messages))
    plane = along_x(column_rows)
    theirs = swap(ours, 1)
    their_teacher = swap(teacher_head, 1)
    their_head = swap(student_head, 1)
    prefetched = [w_gate, w_up, w_down, teacher_head, tokens, final_gain]
    fetched = prefetched if near else []
    split_rows = [((quarter, width + BLOCK), d) for d in [F32] + [BF16] * (size_x - 1)]
    split_dev = [((tok_dev, width + BLOCK), d) for d in [F32] + [BF16] * (size_z - 1)]
    outs = run(
        functools.partial(student_body, devices, order, len(fetched)),
        [
            ((half, 2 * entries), F32),
            ((width, 2 * entries), BF16),
            *split_rows,
            *[(a.shape, a.dtype) for a in fetched],
        ],
        me,
        ours,
        theirs,
        their_head,
        student_head,
        *fetched,
        scratch=[
            pltpu.VMEM((width, entries), BF16),
            pltpu.VMEM((all_rows, 2 * entries), F32),
            pltpu.SemaphoreType.DMA((1 + len(fetched),)),
        ],
        scalars=1,
        far=1 + len(fetched),
        cost=(4 * entries * width * (half + entries), 2 * sum(a.size for a in prefetched)),
        after=[column_rows],
    )
    moved, moved_head, stud_keep, *stud_sends = outs[: 2 + size_x]
    w_gate, w_up, w_down, teacher_head, tokens, final_gain = outs[2 + size_x :] if near else prefetched
    crossed = run(
        pass_body, [(p.shape, p.dtype) for p in plane[1:]], *plane[1:], after=[stud_keep]
    )
    arrived = over_cores([column_rows, *crossed])
    keep, send = run(
        functools.partial(experts_body, slices, len(arrived)),
        [((half, features), F32), ((half, features), BF16)],
        me,
        *arrived,
        w_gate,
        w_up,
        w_down,
        scratch=[pltpu.VMEM((all_rows, features + BLOCK), BF16)],
        scalars=1,
    )
    keep, *sends = add_cores(keep, send, add_split_body)
    summed = from_z(*take(add_x(keep, along(sends), add_split_body)))
    outs = run(
        functools.partial(hidden_body, len(summed) - 1, len(stud_sends)),
        [((tok_dev, features), BF16)] * size_z + [(a.shape, BF16) for a in stud_sends],
        *summed,
        tokens,
        final_gain,
        *stud_sends,
    )
    final_norms, stud_sends = outs[:size_z], outs[size_z:]
    column_rows, *outs = run(
        functools.partial(join_both_body, size_z, size_x),
        [((quarter, features), BF16), *split_dev],
        *along_z(final_norms),
        stud_keep,
        *along(stud_sends),
    )
    student = from_z(*take(outs))
    plane = along_x(column_rows)
    if near:
        (their_teacher,) = run(
            fetch_body,
            [(their_teacher.shape, BF16)],
            their_teacher,
            scratch=[pltpu.SemaphoreType.DMA((1,))],
            far=1,
            cost=(0, 2 * their_teacher.size),
            after=[column_rows],
        )
    keep, *sends = run(
        functools.partial(teacher_body, len(plane)),
        split_rows,
        *plane,
        teacher_head,
        their_teacher,
        moved,
        moved_head,
        scratch=[pltpu.VMEM((half, features), BF16)],
    )
    teacher = from_z(*take(add_x(keep, along(sends), combine_split_body)))
    divergence, grad = run(
        functools.partial(leave_body, len(teacher) - 1),
        [((1, tok_dev), F32), ((tok_dev, width), F32)],
        *teacher,
        *student,
        near_out=False,
    )
    return divergence.reshape(tok_dev), grad


def solution(mesh):
    placed = (
        P(("groups", "expert")),
        P(),
        P(("groups", "expert")),
        P(("groups", "expert")),
        P("expert", None),
        P("expert", None),
        P("expert", None),
        P(),
        P(None, "expert"),
        P("expert"),
        P("groups", "expert"),
        P(None, "expert"),
    )
    return jax.shard_map(
        per_device,
        mesh=mesh,
        in_specs=placed,
        out_specs=(P(("groups", "expert")), P(("groups", "expert"))),
        check_vma=False,
    )
```

```python
import functools

import jax
import jax.numpy as jnp
from jax import lax
from jax.experimental import pallas as pl
from jax.experimental.pallas import tpu as pltpu
from jax.sharding import PartitionSpec as P

FF = 2048
EPSILON = 1e-06
F32 = jnp.float32
BF16 = jnp.bfloat16
BLOCK = 128


def radices(devices):
    bits = devices.bit_length() - 1
    x_bits = (bits - 1) // 3
    return 1 << (bits - 1 - x_bits), 1 << x_bits, 2


def dot(a, b):
    return jnp.dot(a, b, preferred_element_type=F32)


def dot_t(a, b):
    return lax.dot_general(a, b, (((1,), (1,)), ((), ())), preferred_element_type=F32)


def lanes(rows):
    return lax.broadcasted_iota(jnp.int32, (rows, BLOCK), 1)


def pack(columns):
    lane = lanes(columns[0].shape[0])
    block = jnp.zeros(lane.shape, F32)
    for j, column in enumerate(columns):
        block = jnp.where((lane % 32 == j) & (lane < 96), column, block)
    return block


def split(block):
    lane = lanes(block.shape[0])
    high = block.astype(BF16)
    rest = block - high.astype(F32)
    middle = rest.astype(BF16)
    low = (rest - middle.astype(F32)).astype(BF16).astype(F32)
    return jnp.where(lane < 32, high.astype(F32), jnp.where(lane < 64, middle.astype(F32), low)).astype(BF16)


def column(block, j, exact):
    lane = lanes(block.shape[0])
    keep = (lane == j) if exact else (lane % 32 == j)
    return jnp.sum(jnp.where(keep, block, 0.0), axis=1, keepdims=True)


def combine(parts, width):
    blocks = [(ref[:, width:].astype(F32), i == 0) for i, ref in enumerate(parts)]
    tops = [column(b, 0, own) for b, own in blocks]
    top = functools.reduce(jnp.maximum, tops)
    scales = [jnp.exp(t - top) for t in tops]
    totals = [sum(column(b, j, own) * s for (b, own), s in zip(blocks, scales)) for j in (1, 2)]
    values = sum(ref[:, :width].astype(F32) * s for ref, s in zip(parts, scales))
    return values, top, totals


def call(body, outs, *args, scratch=(), scalars=0, after=(), far=0, near=True, near_out=True, limit=12, cost=None, aliases=None):
    smem = pl.BlockSpec(memory_space=pltpu.SMEM)
    vmem = pl.BlockSpec(memory_space=pltpu.VMEM)
    hbm = pl.BlockSpec(memory_space=pltpu.HBM)
    unread = pl.BlockSpec(memory_space=pl.ANY)
    count = len(args)
    middle = count - scalars - far

    def run(*refs):
        body(*refs[:count], *refs[count + len(after) :])

    if near:
        kinds = [None] * scalars + [pltpu.VMEM] * middle + [pltpu.HBM] * far
        args = [a if k is None else pltpu.with_memory_space_constraint(a, k) for a, k in zip(args, kinds)]
    kind = pltpu.VMEM if near and near_out else jax.ShapeDtypeStruct
    return pl.pallas_call(
        run,
        out_shape=[kind(s, d) for s, d in outs],
        in_specs=[smem] * scalars + [vmem] * middle + [hbm] * far + [unread] * len(after),
        out_specs=[vmem] * len(outs),
        scratch_shapes=list(scratch),
        input_output_aliases=aliases or {},
        compiler_params=pltpu.CompilerParams(vmem_limit_bytes=(limit if near else 56) * 2**20),
        cost_estimate=cost and pl.CostEstimate(flops=cost[0], bytes_accessed=cost[1], transcendentals=0),
    )(*args, *after)


def fetch(sources, targets, semaphores):
    copies = [
        pltpu.make_async_copy(source, target, semaphores.at[i])
        for i, (source, target) in enumerate(zip(sources, targets))
    ]
    for copy in copies:
        copy.start()
    return copies


def fetch_body(*refs):
    *refs, semaphores = refs
    for copy in fetch(refs[: len(refs) // 2], refs[len(refs) // 2 :], semaphores):
        copy.wait()


def normed_rows(values, gain):
    return values * lax.rsqrt(jnp.mean(values * values, axis=-1, keepdims=True) + EPSILON) * gain[None, :]


def paired(out):
    return [slice(at, at + 16) for at in range(0, out.shape[0], 16)]


def join_body(turns, *refs):
    *parts, out = refs
    parts = [parts[i] for i in turns]
    for rows, pair in zip(paired(out), zip(*[iter(parts)] * 2)):
        out[rows, :] = jnp.concatenate([p[...].astype(F32) for p in pair]).astype(BF16)


def join_normed_body(turns, gain, *refs):
    *parts, out = refs
    parts = [parts[i] for i in turns]
    for rows, pair in zip(paired(out), zip(*[iter(parts)] * 2)):
        joined = jnp.concatenate([p[...].astype(F32) for p in pair])
        out[rows, :] = normed_rows(joined, gain[...]).astype(BF16)


def experts_body(parts, *refs):
    inputs, (w_gate, w_up, w_down, keep, send, rows_ref) = refs[:parts], refs[parts:]
    count = inputs[0].shape[0]
    features = w_gate.shape[1]
    for i, ref in enumerate(inputs):
        rows_ref[i * count : (i + 1) * count, :] = ref[:, : rows_ref.shape[1]]

    def block(start, size):
        rows = rows_ref[pl.ds(start, size), :]
        gate = dot(rows, w_gate[0])
        up = dot(rows, w_up[0])
        return (gate / (1.0 + jnp.exp(-gate)) * up).astype(BF16)

    half = parts * count // 2
    if half < BLOCK:
        activated = block(0, 2 * half)
        step = 512
        for at in range(0, features, step):
            out = dot(activated, w_down[0, :, at : at + step])
            keep[:, at : at + step] = out[:half]
            send[:, at : at + step] = out[half:].astype(BF16)
    else:
        for h, target in enumerate((keep, send)):

            @pl.loop(0, half // BLOCK)
            def _(i):
                start = pl.multiple_of(i * BLOCK, BLOCK)
                activated = block(h * half + start, BLOCK)
                out = dot(activated, w_down[0])
                target[pl.ds(start, BLOCK), :] = out.astype(target.dtype)


def add_split_body(received, *refs):
    parts, (keep, *sends) = refs[: received + 1], refs[received + 1 :]
    total = sum((ref[...].astype(F32) for ref in parts[1:]), parts[0][...])
    rows = keep.shape[0]
    keep[...] = total[:rows]
    for i, send in enumerate(sends):
        at = (len(sends) - i) * rows
        send[...] = total[at : at + rows].astype(BF16)


def hidden_body(offsets, slices, passing, me, *refs):
    parts, (tokens, gain, ids, scores, *refs) = refs[: len(offsets)], refs[len(offsets) :]
    passed, outs = refs[:passing], refs[passing:]
    rows = tokens.shape[0]
    diagonal = lax.broadcasted_iota(jnp.int32, (rows, rows), 0) == lax.broadcasted_iota(
        jnp.int32, (rows, rows), 1
    )

    def down(values):
        return jnp.sum(jnp.where(diagonal, values, 0.0), axis=1, keepdims=True)

    chosen = [down(ids[k : k + 1, :].astype(F32)) for k in range(ids.shape[0])]
    score = [down(scores[k : k + 1, :]) for k in range(ids.shape[0])]
    whole = sum(score)
    total = tokens[...].astype(F32)
    for ref, offset in zip(parts, offsets):
        expert = ((me[0] ^ offset) // slices).astype(F32)
        weight = sum(jnp.where(c == expert, v, 0.0) for c, v in zip(chosen, score)) / whole
        total = total + ref[...].astype(F32) * weight
    normed = normed_rows(total, gain[...]).astype(BF16)
    for out in outs[: len(outs) - passing]:
        out[...] = normed
    for source, target in zip(passed, outs[len(outs) - passing :]):
        target[...] = source[...]


def student_body(devices, order, prefetched, me, their_map, their_logits, their_head, *refs):
    (map_far, logits_far, head_far, *refs) = refs
    sources, (moved, moved_head, *refs) = refs[:prefetched], refs[prefetched:]
    parts = refs[: len(refs) - prefetched - 5]
    refs = refs[len(parts) :]
    targets, (own_map, logits, head, scratch, semaphores) = refs[:prefetched], refs[prefetched:]
    copies = fetch(
        (map_far, logits_far, head_far, *sources), (own_map, logits, head, *targets), semaphores
    )
    for copy in copies[:3]:
        copy.wait()
    entries = head.shape[1]
    tok_dev = logits.shape[0] // devices
    own, other = (own_map, logits, head), (their_map, their_logits, their_head)
    for i, (places, rows, weights) in enumerate((own, other)):
        cols = slice(i * entries, (i + 1) * entries)
        place = lax.broadcasted_iota(jnp.int32, (entries, entries), 0) == places[...]
        place = jnp.where(place, 1.0, 0.0).astype(BF16)
        scratch[:, cols] = dot_t(rows[...], place)
        moved_head[:, cols] = dot_t(weights[...], place).astype(BF16)
    for slot, offset in enumerate(order):
        source = pl.multiple_of((me[0] ^ offset) * tok_dev, tok_dev)
        moved[slot * tok_dev : (slot + 1) * tok_dev, :] = scratch[pl.ds(source, tok_dev), :]

    width = moved_head.shape[0]
    student_part(moved, moved_head, parts, 0, late(width))

    @pl.when(me[0] % 2 == 1)
    def _():
        student_part(moved, moved_head, parts, late(width), width)

    for copy in copies[3:]:
        copy.wait()


def late(width):
    return width - width // 2 // BLOCK * BLOCK


def student_part(moved, moved_head, targets, start, stop):
    step = min(moved.shape[0], BLOCK)
    for at in range(0, moved.shape[0], step):
        student = moved[at : at + step, :]
        top = jnp.max(student, axis=1, keepdims=True)
        exps = jnp.exp(student - top)
        total = jnp.sum(exps, axis=1, keepdims=True)
        emit(at, step, exps, moved_head, [top, total, jnp.zeros_like(top)], targets, start, stop)


def add_student_body(parts, received, me, moved, moved_head, *refs):
    summands, refs = refs[: received + 1], refs[received + 1 + parts :]
    add_split_body(received, *summands, *refs[:-parts])

    @pl.when(me[0] % 2 == 0)
    def _():
        width = moved_head.shape[0]
        student_part(moved, moved_head, refs[-parts:], late(width), width)


def emit(at, step, exps, head, columns, targets, start, stop):
    stats = pack(columns)
    values = dot_t(exps.astype(BF16), head[start:stop, :])
    width = head.shape[0]
    for i, target in enumerate(targets):
        rows = target.shape[0]
        low, high = max(at, i * rows), min(at + step, (i + 1) * rows)
        if low < high:
            inner, outer = slice(low - at, high - at), slice(low - i * rows, high - i * rows)
            target[outer, start:stop] = values[inner].astype(target.dtype)
            target[outer, width:] = stats[inner] if i == 0 else split(stats[inner])


def teacher_body(parts, *refs):
    inputs, (head, their_head, moved, moved_head, *targets, rows_ref) = refs[:parts], refs[parts:]
    count = inputs[0].shape[0]
    for i, ref in enumerate(inputs):
        rows_ref[i * count : (i + 1) * count, :] = ref[...]
    step = min(parts * count, BLOCK)
    for at in range(0, parts * count, step):
        rows = rows_ref[at : at + step, :]
        teacher = jnp.concatenate([dot(rows, head[...]), dot(rows, their_head[...])], axis=1)
        student = moved[at : at + step, :]
        top = jnp.max(teacher, axis=1, keepdims=True)
        exps = jnp.exp(teacher - top)
        total = jnp.sum(exps, axis=1, keepdims=True)
        cross = jnp.sum(exps * (teacher - student), axis=1, keepdims=True)
        emit(at, step, exps, moved_head, [top, total, cross], targets, 0, moved_head.shape[0])


def combine_split_body(received, *refs):
    parts, (keep, *sends) = refs[: received + 1], refs[received + 1 :]
    width = keep.shape[1] - BLOCK
    values, top, totals = combine(parts, width)
    stats = pack([top, *totals])
    coded = split(stats)
    rows = keep.shape[0]
    keep[:, :width] = values[:rows]
    keep[:, width:] = stats[:rows]
    for i, send in enumerate(sends):
        at = (len(sends) - i) * rows
        inner = slice(at, at + rows)
        send[:, :width] = values[inner].astype(BF16)
        send[:, width:] = coded[inner]


def pass_body(*refs):
    for source, target in zip(refs[: len(refs) // 2], refs[len(refs) // 2 :]):
        target[...] = source[...]


def join_both_body(turns, size_x, *refs):
    parts, refs = refs[: len(turns)], refs[len(turns) :]
    student, (out, *outs) = refs[:size_x], refs[size_x:]
    join_body(turns, *parts, out)
    combine_split_body(size_x - 1, *student, *outs)


def leave_body(received, *refs):
    teacher, refs = refs[: received + 1], refs[received + 1 :]
    student, (divergence, grad) = refs[: received + 1], refs[received + 1 :]
    width = grad.shape[1]
    teach_values, teach_max, (teach_sum, cross_sum) = combine(teacher, width)
    stud_values, stud_max, (stud_sum, _) = combine(student, width)
    grad[...] = stud_values / stud_sum - teach_values / teach_sum
    value = cross_sum / teach_sum - teach_max - jnp.log(teach_sum) + stud_max + jnp.log(stud_sum)
    rows = grad.shape[0]
    diagonal = lax.broadcasted_iota(jnp.int32, (rows, rows), 0) == lax.broadcasted_iota(
        jnp.int32, (rows, rows), 1
    )
    divergence[...] = jnp.sum(jnp.where(diagonal, value, 0.0), axis=0, keepdims=True)


def take(outs):
    return outs[0], outs[1:]


def per_device(
    tokens,
    moe_gain,
    expert_ids,
    gate_scores,
    w_gate,
    w_up,
    w_down,
    final_gain,
    teacher_head,
    vocab_map,
    student_logits,
    student_head,
):
    devices = lax.axis_size("expert")
    size_z, size_x, _ = radices(devices)
    me = lax.axis_index("expert").astype(jnp.int32).reshape(1)
    tok_dev, features = tokens.shape
    slices = FF // w_gate.shape[2]
    width = student_head.shape[0]
    all_rows = devices * tok_dev
    half, quarter = all_rows // 2, all_rows // (2 * size_x)
    entries = student_head.shape[1]
    order = [kz * 2 * size_x + kx * 2 for kx in range(size_x) for kz in range(size_z)]
    near = all_rows <= BLOCK
    run = functools.partial(call, near=near)

    def swap(values, offset):
        return lax.ppermute(values, "expert", [(i, i ^ offset) for i in range(devices)])

    def places(turn):
        return [list(turn).index(kz) if kz else len(turn) for kz in range(size_z)]

    def along_z(rows, turn):
        return [*(swap(rows[kz], kz * 2 * size_x) for kz in turn), rows[0]]

    def along_x(column):
        return [column] + [swap(column, kx * 2) for kx in range(1, size_x)]

    def over_cores(plane):
        return plane + [swap(part, 1) for part in plane]

    def add_x(keep, sends, body, after=()):
        outs = [((tok_dev, keep.shape[1]), d) for d in [F32] + [BF16] * (size_z - 1)]
        return run(functools.partial(body, size_x - 1), outs, keep, *sends, after=after)

    def along(sends):
        return [swap(s, 2 * (size_x - 1 - i)) for i, s in enumerate(sends)]

    def from_z(keep, sends):
        return [keep] + [swap(s, 2 * size_x * (size_z - 1 - i)) for i, s in enumerate(sends)]

    turn = list(range(size_z - 1, 0, -1))
    first_turn = [size_z - 1, *range(1, size_z - 1)]
    parts = along_z([tokens] * size_z, first_turn)
    if near:
        moe_gain, tokens = run(
            fetch_body,
            [(moe_gain.shape, F32), (tokens.shape, BF16)],
            moe_gain,
            tokens,
            scratch=[pltpu.SemaphoreType.DMA((2,))],
            far=2,
            after=parts[:1],
        )
        parts[-1] = tokens
    (column_rows,) = run(
        functools.partial(join_normed_body, places(first_turn)), [((quarter, features), BF16)], moe_gain, *parts)
    plane = along_x(column_rows)
    own_map = vocab_map.reshape(1, -1)
    theirs = [swap(a, 1) for a in (own_map, student_logits, student_head)]
    their_teacher = swap(teacher_head, 1)
    prefetched = [w_gate, w_up, w_down, teacher_head, final_gain, expert_ids.T, gate_scores.T]
    fetched = prefetched if near else []
    split_rows = [((quarter, width + BLOCK), d) for d in [F32] + [BF16] * (size_x - 1)]
    split_dev = [((tok_dev, width + BLOCK), d) for d in [F32] + [BF16] * (size_z - 1)]
    outs = run(
        functools.partial(student_body, devices, order, len(fetched)),
        [
            ((half, 2 * entries), F32),
            ((width, 2 * entries), BF16),
            *split_rows,
            *[(a.shape, a.dtype) for a in fetched],
        ],
        me,
        *theirs,
        own_map,
        student_logits,
        student_head,
        *fetched,
        scratch=[
            pltpu.VMEM((1, entries), jnp.int32),
            pltpu.VMEM((all_rows, entries), BF16),
            pltpu.VMEM((width, entries), BF16),
            pltpu.VMEM((all_rows, 2 * entries), F32),
            pltpu.SemaphoreType.DMA((3 + len(fetched),)),
        ],
        scalars=1,
        far=3 + len(fetched),
        cost=(4 * entries * width * (half + entries), 2 * sum(a.size for a in prefetched)),
        after=[column_rows],
    )
    moved, moved_head, *stud_parts = outs[: 2 + size_x]
    w_gate, w_up, w_down, teacher_head, final_gain, ids, scores = (
        outs[2 + size_x :] if near else prefetched
    )
    crossed = run(
        pass_body, [(p.shape, p.dtype) for p in plane[1:]], *plane[1:], after=[moved]
    )
    arrived = over_cores([column_rows, *crossed])
    keep, send = run(
        functools.partial(experts_body, len(arrived)),
        [((half, features), F32), ((half, features), BF16)],
        *arrived,
        w_gate,
        w_up,
        w_down,
        scratch=[pltpu.VMEM((all_rows, features), BF16)],
    )
    outs = run(
        functools.partial(add_student_body, size_x, 1),
        [((quarter, features), d) for d in [F32] + [BF16] * (size_x - 1)] + split_rows,
        me,
        moved,
        moved_head,
        keep,
        swap(send, 1),
        *stud_parts,
        scalars=1,
        aliases={5 + i: size_x + i for i in range(size_x)},
    )
    keep, *sends = outs[:size_x]
    stud_keep, *stud_sends = outs[size_x:]
    summed = from_z(*take(add_x(keep, along(sends), add_split_body)))
    outs = run(
        functools.partial(
            hidden_body,
            [0] + [2 * size_x * kz for kz in range(size_z - 1, 0, -1)],
            slices,
            len(stud_sends),
        ),
        [((tok_dev, features), BF16)] * size_z + [(a.shape, BF16) for a in stud_sends],
        me,
        *summed,
        tokens,
        final_gain,
        ids,
        scores,
        *stud_sends,
        scalars=1,
    )
    final_norms, stud_sends = outs[:size_z], outs[size_z:]
    column_rows, *outs = run(
        functools.partial(join_both_body, places(turn), size_x),
        [((quarter, features), BF16), *split_dev],
        *along_z(final_norms, turn),
        stud_keep,
        *along(stud_sends),
    )
    student = from_z(*take(outs))
    plane = along_x(column_rows)
    keep, *sends = run(
        functools.partial(teacher_body, len(plane)),
        split_rows,
        *plane,
        teacher_head,
        their_teacher,
        moved,
        moved_head,
        scratch=[pltpu.VMEM((half, features), BF16)],
    )
    teacher = from_z(*take(add_x(keep, along(sends), combine_split_body)))
    divergence, grad = run(
        functools.partial(leave_body, len(teacher) - 1),
        [((1, tok_dev), F32), ((tok_dev, width), F32)],
        *teacher,
        *student,
        near_out=False,
    )
    return divergence.reshape(tok_dev), grad


def solution(mesh):
    placed = (
        P(("groups", "expert")),
        P(),
        P(("groups", "expert")),
        P(("groups", "expert")),
        P("expert", None),
        P("expert", None),
        P("expert", None),
        P(),
        P(None, "expert"),
        P("expert"),
        P("groups", "expert"),
        P(None, "expert"),
    )
    return jax.shard_map(
        per_device,
        mesh=mesh,
        in_specs=placed,
        out_specs=(P(("groups", "expert")), P(("groups", "expert"))),
        check_vma=False,
    )
```

```python
import functools

import jax
import jax.numpy as jnp
from jax import lax
from jax.experimental import pallas as pl
from jax.experimental.pallas import tpu as pltpu
from jax.sharding import PartitionSpec as P

FF = 2048
EPSILON = 1e-06
F32 = jnp.float32
BF16 = jnp.bfloat16
BLOCK = 128


def radices(devices):
    bits = devices.bit_length() - 1
    x_bits = (bits - 1) // 3
    return 1 << (bits - 1 - x_bits), 1 << x_bits, 2


def dot(a, b):
    return jnp.dot(a, b, preferred_element_type=F32)


def dot_t(a, b):
    return lax.dot_general(a, b, (((1,), (1,)), ((), ())), preferred_element_type=F32)


def lanes(rows):
    return lax.broadcasted_iota(jnp.int32, (rows, BLOCK), 1)


def pack(columns):
    lane = lanes(columns[0].shape[0])
    block = jnp.zeros(lane.shape, F32)
    for j, column in enumerate(columns):
        block = jnp.where((lane % 32 == j) & (lane < 96), column, block)
    return block


def split(block):
    lane = lanes(block.shape[0])
    high = block.astype(BF16)
    rest = block - high.astype(F32)
    middle = rest.astype(BF16)
    low = (rest - middle.astype(F32)).astype(BF16).astype(F32)
    return jnp.where(lane < 32, high.astype(F32), jnp.where(lane < 64, middle.astype(F32), low)).astype(BF16)


def column(block, j, exact):
    lane = lanes(block.shape[0])
    keep = (lane == j) if exact else (lane % 32 == j)
    return jnp.sum(jnp.where(keep, block, 0.0), axis=1, keepdims=True)


def combine(parts, width):
    blocks = [(ref[:, width:].astype(F32), i == 0) for i, ref in enumerate(parts)]
    tops = [column(b, 0, own) for b, own in blocks]
    top = functools.reduce(jnp.maximum, tops)
    scales = [jnp.exp(t - top) for t in tops]
    totals = [sum(column(b, j, own) * s for (b, own), s in zip(blocks, scales)) for j in (1, 2)]
    values = sum(ref[:, :width].astype(F32) * s for ref, s in zip(parts, scales))
    return values, top, totals


def call(body, outs, *args, scratch=(), scalars=0, after=(), far=0, near=True, near_out=True, limit=12, cost=None, aliases=None):
    smem = pl.BlockSpec(memory_space=pltpu.SMEM)
    vmem = pl.BlockSpec(memory_space=pltpu.VMEM)
    hbm = pl.BlockSpec(memory_space=pltpu.HBM)
    unread = pl.BlockSpec(memory_space=pl.ANY)
    count = len(args)
    middle = count - scalars - far

    def run(*refs):
        body(*refs[:count], *refs[count + len(after) :])

    if near:
        kinds = [None] * scalars + [pltpu.VMEM] * middle + [pltpu.HBM] * far
        args = [a if k is None else pltpu.with_memory_space_constraint(a, k) for a, k in zip(args, kinds)]
    kind = pltpu.VMEM if near and near_out else jax.ShapeDtypeStruct
    return pl.pallas_call(
        run,
        out_shape=[kind(s, d) for s, d in outs],
        in_specs=[smem] * scalars + [vmem] * middle + [hbm] * far + [unread] * len(after),
        out_specs=[vmem] * len(outs),
        scratch_shapes=list(scratch),
        input_output_aliases=aliases or {},
        compiler_params=pltpu.CompilerParams(vmem_limit_bytes=(limit if near else 56) * 2**20),
        cost_estimate=cost and pl.CostEstimate(flops=cost[0], bytes_accessed=cost[1], transcendentals=0),
    )(*args, *after)


def fetch(sources, targets, semaphores):
    copies = [
        pltpu.make_async_copy(source, target, semaphores.at[i])
        for i, (source, target) in enumerate(zip(sources, targets))
    ]
    for copy in copies:
        copy.start()
    return copies


def fetch_body(*refs):
    *refs, semaphores = refs
    for copy in fetch(refs[: len(refs) // 2], refs[len(refs) // 2 :], semaphores):
        copy.wait()


def normed_rows(values, gain):
    return values * lax.rsqrt(jnp.mean(values * values, axis=-1, keepdims=True) + EPSILON) * gain[None, :]


def paired(out):
    return [slice(at, at + 16) for at in range(0, out.shape[0], 16)]


def join_body(turns, *refs):
    *parts, out = refs
    parts = [parts[i] for i in turns]
    for rows, pair in zip(paired(out), zip(*[iter(parts)] * 2)):
        out[rows, :] = jnp.concatenate([p[...].astype(F32) for p in pair]).astype(BF16)


def join_normed_body(turns, gain, *refs):
    *parts, out = refs
    parts = [parts[i] for i in turns]
    for rows, pair in zip(paired(out), zip(*[iter(parts)] * 2)):
        joined = jnp.concatenate([p[...].astype(F32) for p in pair])
        out[rows, :] = normed_rows(joined, gain[...]).astype(BF16)


def experts_body(parts, *refs):
    inputs, (w_gate, w_up, w_down, keep, send, rows_ref) = refs[:parts], refs[parts:]
    count = inputs[0].shape[0]
    features = w_gate.shape[1]
    for i, ref in enumerate(inputs):
        rows_ref[i * count : (i + 1) * count, :] = ref[:, : rows_ref.shape[1]]

    def block(start, size):
        rows = rows_ref[pl.ds(start, size), :]
        gate = dot(rows, w_gate[0])
        up = dot(rows, w_up[0])
        return (gate / (1.0 + jnp.exp(-gate)) * up).astype(BF16)

    half = parts * count // 2
    if half < BLOCK:
        activated = block(0, 2 * half)
        step = 512
        for at in range(0, features, step):
            out = dot(activated, w_down[0, :, at : at + step])
            keep[:, at : at + step] = out[:half]
            send[:, at : at + step] = out[half:].astype(BF16)
    else:
        for h, target in enumerate((keep, send)):

            @pl.loop(0, half // BLOCK)
            def _(i):
                start = pl.multiple_of(i * BLOCK, BLOCK)
                activated = block(h * half + start, BLOCK)
                out = dot(activated, w_down[0])
                target[pl.ds(start, BLOCK), :] = out.astype(target.dtype)


def add_split_body(received, *refs):
    parts, (keep, *sends) = refs[: received + 1], refs[received + 1 :]
    total = sum((ref[...].astype(F32) for ref in parts[1:]), parts[0][...])
    rows = keep.shape[0]
    keep[...] = total[:rows]
    for i, send in enumerate(sends):
        at = (len(sends) - i) * rows
        send[...] = total[at : at + rows].astype(BF16)


def hidden_body(offsets, slices, passing, me, *refs):
    parts, (tokens, gain, ids, scores, *refs) = refs[: len(offsets)], refs[len(offsets) :]
    passed, outs = refs[:passing], refs[passing:]
    rows = tokens.shape[0]
    diagonal = lax.broadcasted_iota(jnp.int32, (rows, rows), 0) == lax.broadcasted_iota(
        jnp.int32, (rows, rows), 1
    )

    def down(values):
        return jnp.sum(jnp.where(diagonal, values, 0.0), axis=1, keepdims=True)

    chosen = [down(ids[k : k + 1, :].astype(F32)) for k in range(ids.shape[0])]
    score = [down(scores[k : k + 1, :]) for k in range(ids.shape[0])]
    whole = sum(score)
    total = tokens[...].astype(F32)
    for ref, offset in zip(parts, offsets):
        expert = ((me[0] ^ offset) // slices).astype(F32)
        weight = sum(jnp.where(c == expert, v, 0.0) for c, v in zip(chosen, score)) / whole
        total = total + ref[...].astype(F32) * weight
    normed = normed_rows(total, gain[...]).astype(BF16)
    for out in outs[: len(outs) - passing]:
        out[...] = normed
    for source, target in zip(passed, outs[len(outs) - passing :]):
        target[...] = source[...]


def student_body(devices, order, prefetched, me, their_map, their_logits, their_head, *refs):
    (map_far, logits_far, head_far, *refs) = refs
    sources, (moved, moved_head, *refs) = refs[:prefetched], refs[prefetched:]
    parts = refs[: len(refs) - prefetched - 5]
    refs = refs[len(parts) :]
    targets, (own_map, logits, head, scratch, semaphores) = refs[:prefetched], refs[prefetched:]
    copies = fetch(
        (map_far, logits_far, head_far, *sources), (own_map, logits, head, *targets), semaphores
    )
    for copy in copies[:3]:
        copy.wait()
    entries = head.shape[1]
    tok_dev = logits.shape[0] // devices
    own, other = (own_map, logits, head), (their_map, their_logits, their_head)
    for i, (places, rows, weights) in enumerate((own, other)):
        cols = slice(i * entries, (i + 1) * entries)
        place = lax.broadcasted_iota(jnp.int32, (entries, entries), 0) == places[...]
        place = jnp.where(place, 1.0, 0.0).astype(BF16)
        scratch[:, cols] = dot_t(rows[...], place)
        moved_head[:, cols] = dot_t(weights[...], place).astype(BF16)
    for slot, offset in enumerate(order):
        source = pl.multiple_of((me[0] ^ offset) * tok_dev, tok_dev)
        moved[slot * tok_dev : (slot + 1) * tok_dev, :] = scratch[pl.ds(source, tok_dev), :]

    width = moved_head.shape[0]
    student_part(moved, moved_head, parts, 0, late(width))

    @pl.when(me[0] % 2 == 1)
    def _():
        student_part(moved, moved_head, parts, late(width), width)

    for copy in copies[3:]:
        copy.wait()


def late(width):
    return width - width // 2 // BLOCK * BLOCK


def student_part(moved, moved_head, targets, start, stop):
    step = min(moved.shape[0], BLOCK)
    for at in range(0, moved.shape[0], step):
        student = moved[at : at + step, :]
        top = jnp.max(student, axis=1, keepdims=True)
        exps = jnp.exp(student - top)
        total = jnp.sum(exps, axis=1, keepdims=True)
        emit(at, step, exps, moved_head, [top, total, jnp.zeros_like(top)], targets, start, stop)


def add_student_body(parts, received, me, moved, moved_head, *refs):
    summands, refs = refs[: received + 1], refs[received + 1 + parts :]
    add_split_body(received, *summands, *refs[:-parts])

    @pl.when(me[0] % 2 == 0)
    def _():
        width = moved_head.shape[0]
        student_part(moved, moved_head, refs[-parts:], late(width), width)


def emit(at, step, exps, head, columns, targets, start, stop):
    stats = pack(columns)
    values = dot_t(exps.astype(BF16), head[start:stop, :])
    width = head.shape[0]
    for i, target in enumerate(targets):
        rows = target.shape[0]
        low, high = max(at, i * rows), min(at + step, (i + 1) * rows)
        if low < high:
            inner, outer = slice(low - at, high - at), slice(low - i * rows, high - i * rows)
            target[outer, start:stop] = values[inner].astype(target.dtype)
            target[outer, width:] = stats[inner] if i == 0 else split(stats[inner])


def teacher_body(parts, *refs):
    inputs, (head, their_head, moved, moved_head, *targets, rows_ref) = refs[:parts], refs[parts:]
    count = inputs[0].shape[0]
    for i, ref in enumerate(inputs):
        rows_ref[i * count : (i + 1) * count, :] = ref[...]
    step = min(parts * count, BLOCK)
    for at in range(0, parts * count, step):
        rows = rows_ref[at : at + step, :]
        teacher = jnp.concatenate([dot(rows, head[...]), dot(rows, their_head[...])], axis=1)
        student = moved[at : at + step, :]
        top = jnp.max(teacher, axis=1, keepdims=True)
        exps = jnp.exp(teacher - top)
        total = jnp.sum(exps, axis=1, keepdims=True)
        cross = jnp.sum(exps * (teacher - student), axis=1, keepdims=True)
        emit(at, step, exps, moved_head, [top, total, cross], targets, 0, moved_head.shape[0])


def combine_split_body(received, *refs):
    parts, (keep, *sends) = refs[: received + 1], refs[received + 1 :]
    width = keep.shape[1] - BLOCK
    values, top, totals = combine(parts, width)
    stats = pack([top, *totals])
    coded = split(stats)
    rows = keep.shape[0]
    keep[:, :width] = values[:rows]
    keep[:, width:] = stats[:rows]
    for i, send in enumerate(sends):
        at = (len(sends) - i) * rows
        inner = slice(at, at + rows)
        send[:, :width] = values[inner].astype(BF16)
        send[:, width:] = coded[inner]


def pass_body(*refs):
    for source, target in zip(refs[: len(refs) // 2], refs[len(refs) // 2 :]):
        target[...] = source[...]


def join_both_body(turns, size_x, *refs):
    parts, refs = refs[: len(turns)], refs[len(turns) :]
    student, (out, *outs) = refs[:size_x], refs[size_x:]
    join_body(turns, *parts, out)
    combine_split_body(size_x - 1, *student, *outs)


def leave_body(received, *refs):
    teacher, refs = refs[: received + 1], refs[received + 1 :]
    student, (divergence, grad) = refs[: received + 1], refs[received + 1 :]
    width = grad.shape[1]
    teach_values, teach_max, (teach_sum, cross_sum) = combine(teacher, width)
    stud_values, stud_max, (stud_sum, _) = combine(student, width)
    grad[...] = stud_values / stud_sum - teach_values / teach_sum
    value = cross_sum / teach_sum - teach_max - jnp.log(teach_sum) + stud_max + jnp.log(stud_sum)
    rows = grad.shape[0]
    diagonal = lax.broadcasted_iota(jnp.int32, (rows, rows), 0) == lax.broadcasted_iota(
        jnp.int32, (rows, rows), 1
    )
    divergence[...] = jnp.sum(jnp.where(diagonal, value, 0.0), axis=0, keepdims=True)


def take(outs):
    return outs[0], outs[1:]


def per_device(
    tokens,
    moe_gain,
    expert_ids,
    gate_scores,
    w_gate,
    w_up,
    w_down,
    final_gain,
    teacher_head,
    vocab_map,
    student_logits,
    student_head,
):
    devices = lax.axis_size("expert")
    size_z, size_x, _ = radices(devices)
    me = lax.axis_index("expert").astype(jnp.int32).reshape(1)
    tok_dev, features = tokens.shape
    slices = FF // w_gate.shape[2]
    width = student_head.shape[0]
    all_rows = devices * tok_dev
    half, quarter = all_rows // 2, all_rows // (2 * size_x)
    entries = student_head.shape[1]
    order = [kz * 2 * size_x + kx * 2 for kx in range(size_x) for kz in range(size_z)]
    near = all_rows <= BLOCK
    run = functools.partial(call, near=near)

    def swap(values, offset):
        return lax.ppermute(values, "expert", [(i, i ^ offset) for i in range(devices)])

    def places(turn):
        return [list(turn).index(kz) if kz else len(turn) for kz in range(size_z)]

    def along_z(rows, turn):
        return [*(swap(rows[kz], kz * 2 * size_x) for kz in turn), rows[0]]

    def along_x(column):
        return [column] + [swap(column, kx * 2) for kx in range(1, size_x)]

    def over_cores(plane):
        return plane + [swap(part, 1) for part in plane]

    def add_x(keep, sends, body, after=()):
        outs = [((tok_dev, keep.shape[1]), d) for d in [F32] + [BF16] * (size_z - 1)]
        return run(functools.partial(body, size_x - 1), outs, keep, *sends, after=after)

    def along(sends):
        return [swap(s, 2 * (size_x - 1 - i)) for i, s in enumerate(sends)]

    def from_z(keep, sends):
        return [keep] + [swap(s, 2 * size_x * (size_z - 1 - i)) for i, s in enumerate(sends)]

    turn = list(range(size_z - 1, 0, -1))
    first_turn = [size_z - 1, *range(1, size_z - 1)]
    parts = along_z([tokens] * size_z, first_turn)
    if near:
        moe_gain, tokens = run(
            fetch_body,
            [(moe_gain.shape, F32), (tokens.shape, BF16)],
            moe_gain,
            tokens,
            scratch=[pltpu.SemaphoreType.DMA((2,))],
            far=2,
            after=parts[:1],
        )
        parts[-1] = tokens
    (column_rows,) = run(
        functools.partial(join_normed_body, places(first_turn)), [((quarter, features), BF16)], moe_gain, *parts)
    plane = along_x(column_rows)
    own_map = vocab_map.reshape(1, -1)
    theirs = [swap(a, 1) for a in (own_map, student_logits, student_head)]
    their_teacher = swap(teacher_head, 1)
    prefetched = [w_gate, w_up, w_down, final_gain, expert_ids.T, gate_scores.T]
    fetched = prefetched if near else []
    split_rows = [((quarter, width + BLOCK), d) for d in [F32] + [BF16] * (size_x - 1)]
    split_dev = [((tok_dev, width + BLOCK), d) for d in [F32] + [BF16] * (size_z - 1)]
    outs = run(
        functools.partial(student_body, devices, order, len(fetched)),
        [
            ((half, 2 * entries), F32),
            ((width, 2 * entries), BF16),
            *split_rows,
            *[(a.shape, a.dtype) for a in fetched],
        ],
        me,
        *theirs,
        own_map,
        student_logits,
        student_head,
        *fetched,
        scratch=[
            pltpu.VMEM((1, entries), jnp.int32),
            pltpu.VMEM((all_rows, entries), BF16),
            pltpu.VMEM((width, entries), BF16),
            pltpu.VMEM((all_rows, 2 * entries), F32),
            pltpu.SemaphoreType.DMA((3 + len(fetched),)),
        ],
        scalars=1,
        far=3 + len(fetched),
        cost=(4 * entries * width * (half + entries), 2 * sum(a.size for a in prefetched)),
        after=[column_rows],
    )
    moved, moved_head, *stud_parts = outs[: 2 + size_x]
    w_gate, w_up, w_down, final_gain, ids, scores = (
        outs[2 + size_x :] if near else prefetched
    )
    crossed = run(
        pass_body, [(p.shape, p.dtype) for p in plane[1:]], *plane[1:], after=[moved]
    )
    arrived = over_cores([column_rows, *crossed])
    keep, send = run(
        functools.partial(experts_body, len(arrived)),
        [((half, features), F32), ((half, features), BF16)],
        *arrived,
        w_gate,
        w_up,
        w_down,
        scratch=[pltpu.VMEM((all_rows, features), BF16)],
    )
    outs = run(
        functools.partial(add_student_body, size_x, 1),
        [((quarter, features), d) for d in [F32] + [BF16] * (size_x - 1)] + split_rows,
        me,
        moved,
        moved_head,
        keep,
        swap(send, 1),
        *stud_parts,
        scalars=1,
        aliases={5 + i: size_x + i for i in range(size_x)},
    )
    keep, *sends = outs[:size_x]
    stud_keep, *stud_sends = outs[size_x:]
    summed = from_z(*take(add_x(keep, along(sends), add_split_body)))
    outs = run(
        functools.partial(
            hidden_body,
            [0] + [2 * size_x * kz for kz in range(size_z - 1, 0, -1)],
            slices,
            len(stud_sends),
        ),
        [((tok_dev, features), BF16)] * size_z + [(a.shape, BF16) for a in stud_sends],
        me,
        *summed,
        tokens,
        final_gain,
        ids,
        scores,
        *stud_sends,
        scalars=1,
    )
    final_norms, stud_sends = outs[:size_z], outs[size_z:]
    column_rows, *outs = run(
        functools.partial(join_both_body, places(turn), size_x),
        [((quarter, features), BF16), *split_dev],
        *along_z(final_norms, turn),
        stud_keep,
        *along(stud_sends),
    )
    student = from_z(*take(outs))
    plane = along_x(column_rows)
    if near:
        (teacher_head,) = run(
            fetch_body,
            [(teacher_head.shape, BF16)],
            teacher_head,
            scratch=[pltpu.SemaphoreType.DMA((1,))],
            far=1,
            cost=(0, 2 * teacher_head.size),
            after=[column_rows],
        )
    keep, *sends = run(
        functools.partial(teacher_body, len(plane)),
        split_rows,
        *plane,
        teacher_head,
        their_teacher,
        moved,
        moved_head,
        scratch=[pltpu.VMEM((half, features), BF16)],
    )
    teacher = from_z(*take(add_x(keep, along(sends), combine_split_body)))
    divergence, grad = run(
        functools.partial(leave_body, len(teacher) - 1),
        [((1, tok_dev), F32), ((tok_dev, width), F32)],
        *teacher,
        *student,
        near_out=False,
    )
    return divergence.reshape(tok_dev), grad


def solution(mesh):
    placed = (
        P(("groups", "expert")),
        P(),
        P(("groups", "expert")),
        P(("groups", "expert")),
        P("expert", None),
        P("expert", None),
        P("expert", None),
        P(),
        P(None, "expert"),
        P("expert"),
        P("groups", "expert"),
        P(None, "expert"),
    )
    return jax.shard_map(
        per_device,
        mesh=mesh,
        in_specs=placed,
        out_specs=(P(("groups", "expert")), P(("groups", "expert"))),
        check_vma=False,
    )
```

```python
import functools

import jax
import jax.numpy as jnp
from jax import lax
from jax.experimental import pallas as pl
from jax.experimental.pallas import tpu as pltpu
from jax.sharding import PartitionSpec as P

FF = 2048
EPSILON = 1e-06
F32 = jnp.float32
BF16 = jnp.bfloat16
BLOCK = 128


def radices(devices):
    bits = devices.bit_length() - 1
    x_bits = (bits - 1) // 3
    return 1 << (bits - 1 - x_bits), 1 << x_bits, 2


def dot(a, b):
    return jnp.dot(a, b, preferred_element_type=F32)


def dot_t(a, b):
    return lax.dot_general(a, b, (((1,), (1,)), ((), ())), preferred_element_type=F32)


def lanes(rows):
    return lax.broadcasted_iota(jnp.int32, (rows, BLOCK), 1)


def pack(columns):
    lane = lanes(columns[0].shape[0])
    block = jnp.zeros(lane.shape, F32)
    for j, column in enumerate(columns):
        block = jnp.where((lane % 32 == j) & (lane < 96), column, block)
    return block


def split(block):
    lane = lanes(block.shape[0])
    high = block.astype(BF16)
    rest = block - high.astype(F32)
    middle = rest.astype(BF16)
    low = (rest - middle.astype(F32)).astype(BF16).astype(F32)
    return jnp.where(lane < 32, high.astype(F32), jnp.where(lane < 64, middle.astype(F32), low)).astype(BF16)


def column(block, j, exact):
    lane = lanes(block.shape[0])
    keep = (lane == j) if exact else (lane % 32 == j)
    return jnp.sum(jnp.where(keep, block, 0.0), axis=1, keepdims=True)


def combine(parts, width):
    blocks = [(ref[:, width:].astype(F32), i == 0) for i, ref in enumerate(parts)]
    tops = [column(b, 0, own) for b, own in blocks]
    top = functools.reduce(jnp.maximum, tops)
    scales = [jnp.exp(t - top) for t in tops]
    totals = [sum(column(b, j, own) * s for (b, own), s in zip(blocks, scales)) for j in (1, 2)]
    values = sum(ref[:, :width].astype(F32) * s for ref, s in zip(parts, scales))
    return values, top, totals


def call(body, outs, *args, scratch=(), scalars=0, after=(), far=0, near=True, near_out=True, limit=12, cost=None, aliases=None):
    smem = pl.BlockSpec(memory_space=pltpu.SMEM)
    vmem = pl.BlockSpec(memory_space=pltpu.VMEM)
    hbm = pl.BlockSpec(memory_space=pltpu.HBM)
    unread = pl.BlockSpec(memory_space=pl.ANY)
    count = len(args)
    middle = count - scalars - far

    def run(*refs):
        body(*refs[:count], *refs[count + len(after) :])

    if near:
        kinds = [None] * scalars + [pltpu.VMEM] * middle + [pltpu.HBM] * far
        args = [a if k is None else pltpu.with_memory_space_constraint(a, k) for a, k in zip(args, kinds)]
    kind = pltpu.VMEM if near and near_out else jax.ShapeDtypeStruct
    return pl.pallas_call(
        run,
        out_shape=[kind(s, d) for s, d in outs],
        in_specs=[smem] * scalars + [vmem] * middle + [hbm] * far + [unread] * len(after),
        out_specs=[vmem] * len(outs),
        scratch_shapes=list(scratch),
        input_output_aliases=aliases or {},
        compiler_params=pltpu.CompilerParams(vmem_limit_bytes=(limit if near else 56) * 2**20),
        cost_estimate=cost and pl.CostEstimate(flops=cost[0], bytes_accessed=cost[1], transcendentals=0),
    )(*args, *after)


def fetch(sources, targets, semaphores):
    copies = [
        pltpu.make_async_copy(source, target, semaphores.at[i])
        for i, (source, target) in enumerate(zip(sources, targets))
    ]
    for copy in copies:
        copy.start()
    return copies


def fetch_body(*refs):
    *refs, semaphores = refs
    for copy in fetch(refs[: len(refs) // 2], refs[len(refs) // 2 :], semaphores):
        copy.wait()


def normed_rows(values, gain):
    return values * lax.rsqrt(jnp.mean(values * values, axis=-1, keepdims=True) + EPSILON) * gain[None, :]


def paired(out):
    return [slice(at, at + 16) for at in range(0, out.shape[0], 16)]


def join_body(turns, *refs):
    *parts, out = refs
    parts = [parts[i] for i in turns]
    for rows, pair in zip(paired(out), zip(*[iter(parts)] * 2)):
        out[rows, :] = jnp.concatenate([p[...].astype(F32) for p in pair]).astype(BF16)


def join_normed_body(turns, gain, *refs):
    *parts, out = refs
    parts = [parts[i] for i in turns]
    for rows, pair in zip(paired(out), zip(*[iter(parts)] * 2)):
        joined = jnp.concatenate([p[...].astype(F32) for p in pair])
        out[rows, :] = normed_rows(joined, gain[...]).astype(BF16)


def experts_body(parts, *refs):
    inputs, (w_gate, w_up, w_down, keep, send, rows_ref) = refs[:parts], refs[parts:]
    count = inputs[0].shape[0]
    features = w_gate.shape[1]
    for i, ref in enumerate(inputs):
        rows_ref[i * count : (i + 1) * count, :] = ref[:, : rows_ref.shape[1]]

    def block(start, size):
        rows = rows_ref[pl.ds(start, size), :]
        gate = dot(rows, w_gate[0])
        up = dot(rows, w_up[0])
        return (gate / (1.0 + jnp.exp(-gate)) * up).astype(BF16)

    half = parts * count // 2
    if half < BLOCK:
        activated = block(0, 2 * half)
        step = 512
        for at in range(0, features, step):
            out = dot(activated, w_down[0, :, at : at + step])
            keep[:, at : at + step] = out[:half]
            send[:, at : at + step] = out[half:].astype(BF16)
    else:
        for h, target in enumerate((keep, send)):

            @pl.loop(0, half // BLOCK)
            def _(i):
                start = pl.multiple_of(i * BLOCK, BLOCK)
                activated = block(h * half + start, BLOCK)
                out = dot(activated, w_down[0])
                target[pl.ds(start, BLOCK), :] = out.astype(target.dtype)


def add_split_body(received, *refs):
    parts, (keep, *sends) = refs[: received + 1], refs[received + 1 :]
    total = sum((ref[...].astype(F32) for ref in parts[1:]), parts[0][...])
    rows = keep.shape[0]
    keep[...] = total[:rows]
    for i, send in enumerate(sends):
        at = (len(sends) - i) * rows
        send[...] = total[at : at + rows].astype(BF16)


def add_half_body(received, upper, keep, *refs):
    parts, outs = refs[:received], refs[received:]
    half = keep.shape[0] // 2
    total = keep[half:, :] if upper else keep[:half, :]
    total = sum((ref[...].astype(F32) for ref in parts), total)
    rows = outs[0].shape[0]
    for i, out in enumerate(outs):
        at = (len(outs) - 1 - i) * rows
        out[...] = total[at : at + rows].astype(out.dtype)


def hidden_body(offsets, slices, passing, me, *refs):
    parts, (tokens, gain, ids, scores, *refs) = refs[: len(offsets)], refs[len(offsets) :]
    passed, outs = refs[:passing], refs[passing:]
    rows = tokens.shape[0]
    diagonal = lax.broadcasted_iota(jnp.int32, (rows, rows), 0) == lax.broadcasted_iota(
        jnp.int32, (rows, rows), 1
    )

    def down(values):
        return jnp.sum(jnp.where(diagonal, values, 0.0), axis=1, keepdims=True)

    chosen = [down(ids[k : k + 1, :].astype(F32)) for k in range(ids.shape[0])]
    score = [down(scores[k : k + 1, :]) for k in range(ids.shape[0])]
    whole = sum(score)
    total = tokens[...].astype(F32)
    for ref, offset in zip(parts, offsets):
        expert = ((me[0] ^ offset) // slices).astype(F32)
        weight = sum(jnp.where(c == expert, v, 0.0) for c, v in zip(chosen, score)) / whole
        total = total + ref[...].astype(F32) * weight
    normed = normed_rows(total, gain[...]).astype(BF16)
    for out in outs[: len(outs) - passing]:
        out[...] = normed
    for source, target in zip(passed, outs[len(outs) - passing :]):
        target[...] = source[...]


def student_body(devices, order, prefetched, me, their_map, their_logits, their_head, *refs):
    (map_far, logits_far, head_far, *refs) = refs
    sources, (moved, moved_head, *refs) = refs[:prefetched], refs[prefetched:]
    parts = refs[: len(refs) - prefetched - 5]
    refs = refs[len(parts) :]
    targets, (own_map, logits, head, scratch, semaphores) = refs[:prefetched], refs[prefetched:]
    copies = fetch(
        (map_far, logits_far, head_far, *sources), (own_map, logits, head, *targets), semaphores
    )
    for copy in copies[:3]:
        copy.wait()
    entries = head.shape[1]
    tok_dev = logits.shape[0] // devices
    own, other = (own_map, logits, head), (their_map, their_logits, their_head)
    for i, (places, rows, weights) in enumerate((own, other)):
        cols = slice(i * entries, (i + 1) * entries)
        place = lax.broadcasted_iota(jnp.int32, (entries, entries), 0) == places[...]
        place = jnp.where(place, 1.0, 0.0).astype(BF16)
        scratch[:, cols] = dot_t(rows[...], place)
        moved_head[:, cols] = dot_t(weights[...], place).astype(BF16)
    for slot, offset in enumerate(order):
        source = pl.multiple_of((me[0] ^ offset) * tok_dev, tok_dev)
        moved[slot * tok_dev : (slot + 1) * tok_dev, :] = scratch[pl.ds(source, tok_dev), :]

    width = moved_head.shape[0]
    student_part(moved, moved_head, parts, 0, late(width))

    @pl.when(me[0] % 2 == 1)
    def _():
        student_part(moved, moved_head, parts, late(width), width)

    for copy in copies[3:]:
        copy.wait()


def late(width):
    return width - width // 8 // BLOCK * BLOCK


def student_part(moved, moved_head, targets, start, stop):
    step = min(moved.shape[0], BLOCK)
    for at in range(0, moved.shape[0], step):
        student = moved[at : at + step, :]
        top = jnp.max(student, axis=1, keepdims=True)
        exps = jnp.exp(student - top)
        total = jnp.sum(exps, axis=1, keepdims=True)
        emit(at, step, exps, moved_head, [top, total, jnp.zeros_like(top)], targets, start, stop)


def add_student_body(parts, received, me, moved, moved_head, *refs):
    summands, refs = refs[: received + 1], refs[received + 1 + parts :]
    total = sum((ref[...].astype(F32) for ref in summands[1:]), summands[0][...])
    keep, *sends = refs[:-parts]
    rows = keep.shape[0]
    keep[...] = total[:rows]
    for i, send in enumerate(sends):
        at = (len(sends) // 2 - i // 2) * rows + (1 - i % 2) * rows // 2
        send[...] = total[at : at + rows // 2].astype(BF16)

    @pl.when(me[0] % 2 == 0)
    def _():
        width = moved_head.shape[0]
        student_part(moved, moved_head, refs[-parts:], late(width), width)


def emit(at, step, exps, head, columns, targets, start, stop):
    stats = pack(columns)
    values = dot_t(exps.astype(BF16), head[start:stop, :])
    width = head.shape[0]
    for i, target in enumerate(targets):
        rows = target.shape[0]
        low, high = max(at, i * rows), min(at + step, (i + 1) * rows)
        if low < high:
            inner, outer = slice(low - at, high - at), slice(low - i * rows, high - i * rows)
            target[outer, start:stop] = values[inner].astype(target.dtype)
            target[outer, width:] = stats[inner] if i == 0 else split(stats[inner])


def teacher_body(parts, *refs):
    inputs, (head, their_head, moved, moved_head, *targets, rows_ref) = refs[:parts], refs[parts:]
    count = inputs[0].shape[0]
    for i, ref in enumerate(inputs):
        rows_ref[i * count : (i + 1) * count, :] = ref[...]
    step = min(parts * count, BLOCK)
    for at in range(0, parts * count, step):
        rows = rows_ref[at : at + step, :]
        teacher = jnp.concatenate([dot(rows, head[...]), dot(rows, their_head[...])], axis=1)
        student = moved[at : at + step, :]
        top = jnp.max(teacher, axis=1, keepdims=True)
        exps = jnp.exp(teacher - top)
        total = jnp.sum(exps, axis=1, keepdims=True)
        cross = jnp.sum(exps * (teacher - student), axis=1, keepdims=True)
        emit(at, step, exps, moved_head, [top, total, cross], targets, 0, moved_head.shape[0])


def combine_split_body(received, *refs):
    parts, (keep, *sends) = refs[: received + 1], refs[received + 1 :]
    width = keep.shape[1] - BLOCK
    values, top, totals = combine(parts, width)
    stats = pack([top, *totals])
    coded = split(stats)
    rows = keep.shape[0]
    keep[:, :width] = values[:rows]
    keep[:, width:] = stats[:rows]
    for i, send in enumerate(sends):
        at = (len(sends) - i) * rows
        inner = slice(at, at + rows)
        send[:, :width] = values[inner].astype(BF16)
        send[:, width:] = coded[inner]


def pass_body(*refs):
    for source, target in zip(refs[: len(refs) // 2], refs[len(refs) // 2 :]):
        target[...] = source[...]


def join_both_body(turns, size_x, *refs):
    parts, refs = refs[: len(turns)], refs[len(turns) :]
    student, (out, *outs) = refs[:size_x], refs[size_x:]
    join_body(turns, *parts, out)
    combine_split_body(size_x - 1, *student, *outs)


def leave_body(received, *refs):
    teacher, refs = refs[: received + 1], refs[received + 1 :]
    student, (divergence, grad) = refs[: received + 1], refs[received + 1 :]
    width = grad.shape[1]
    teach_values, teach_max, (teach_sum, cross_sum) = combine(teacher, width)
    stud_values, stud_max, (stud_sum, _) = combine(student, width)
    grad[...] = stud_values / stud_sum - teach_values / teach_sum
    value = cross_sum / teach_sum - teach_max - jnp.log(teach_sum) + stud_max + jnp.log(stud_sum)
    rows = grad.shape[0]
    diagonal = lax.broadcasted_iota(jnp.int32, (rows, rows), 0) == lax.broadcasted_iota(
        jnp.int32, (rows, rows), 1
    )
    divergence[...] = jnp.sum(jnp.where(diagonal, value, 0.0), axis=0, keepdims=True)


def take(outs):
    return outs[0], outs[1:]


def per_device(
    tokens,
    moe_gain,
    expert_ids,
    gate_scores,
    w_gate,
    w_up,
    w_down,
    final_gain,
    teacher_head,
    vocab_map,
    student_logits,
    student_head,
):
    devices = lax.axis_size("expert")
    size_z, size_x, _ = radices(devices)
    me = lax.axis_index("expert").astype(jnp.int32).reshape(1)
    tok_dev, features = tokens.shape
    slices = FF // w_gate.shape[2]
    width = student_head.shape[0]
    all_rows = devices * tok_dev
    half, quarter = all_rows // 2, all_rows // (2 * size_x)
    entries = student_head.shape[1]
    order = [kz * 2 * size_x + kx * 2 for kx in range(size_x) for kz in range(size_z)]
    near = all_rows <= BLOCK
    run = functools.partial(call, near=near)

    def swap(values, offset):
        return lax.ppermute(values, "expert", [(i, i ^ offset) for i in range(devices)])

    def places(turn):
        return [list(turn).index(kz) if kz else len(turn) for kz in range(size_z)]

    def along_z(rows, turn):
        return [*(swap(rows[kz], kz * 2 * size_x) for kz in turn), rows[0]]

    def along_x(column):
        return [column] + [swap(column, kx * 2) for kx in range(1, size_x)]

    def over_cores(plane):
        return plane + [swap(part, 1) for part in plane]

    def add_x(keep, sends, body, after=()):
        outs = [((tok_dev, keep.shape[1]), d) for d in [F32] + [BF16] * (size_z - 1)]
        return run(functools.partial(body, size_x - 1), outs, keep, *sends, after=after)

    def along(sends):
        return [swap(s, 2 * (size_x - 1 - i)) for i, s in enumerate(sends)]

    def from_z(keep, sends):
        return [keep] + [swap(s, 2 * size_x * (size_z - 1 - i)) for i, s in enumerate(sends)]

    turn = list(range(size_z - 1, 0, -1))
    first_turn = [size_z - 1, *range(1, size_z - 1)]
    parts = along_z([tokens] * size_z, first_turn)
    if near:
        moe_gain, tokens = run(
            fetch_body,
            [(moe_gain.shape, F32), (tokens.shape, BF16)],
            moe_gain,
            tokens,
            scratch=[pltpu.SemaphoreType.DMA((2,))],
            far=2,
            after=parts[:1],
        )
        parts[-1] = tokens
    (column_rows,) = run(
        functools.partial(join_normed_body, places(first_turn)), [((quarter, features), BF16)], moe_gain, *parts)
    plane = along_x(column_rows)
    own_map = vocab_map.reshape(1, -1)
    theirs = [swap(a, 1) for a in (own_map, student_logits, student_head)]
    their_teacher = swap(teacher_head, 1)
    prefetched = [w_gate, w_up, w_down, final_gain, expert_ids.T, gate_scores.T]
    fetched = prefetched if near else []
    split_rows = [((quarter, width + BLOCK), d) for d in [F32] + [BF16] * (size_x - 1)]
    split_dev = [((tok_dev, width + BLOCK), d) for d in [F32] + [BF16] * (size_z - 1)]
    outs = run(
        functools.partial(student_body, devices, order, len(fetched)),
        [
            ((half, 2 * entries), F32),
            ((width, 2 * entries), BF16),
            *split_rows,
            *[(a.shape, a.dtype) for a in fetched],
        ],
        me,
        *theirs,
        own_map,
        student_logits,
        student_head,
        *fetched,
        scratch=[
            pltpu.VMEM((1, entries), jnp.int32),
            pltpu.VMEM((all_rows, entries), BF16),
            pltpu.VMEM((width, entries), BF16),
            pltpu.VMEM((all_rows, 2 * entries), F32),
            pltpu.SemaphoreType.DMA((3 + len(fetched),)),
        ],
        scalars=1,
        far=3 + len(fetched),
        cost=(4 * entries * width * (half + entries), 2 * sum(a.size for a in prefetched)),
        after=[column_rows],
    )
    moved, moved_head, *stud_parts = outs[: 2 + size_x]
    w_gate, w_up, w_down, final_gain, ids, scores = (
        outs[2 + size_x :] if near else prefetched
    )
    crossed = run(
        pass_body, [(p.shape, p.dtype) for p in plane[1:]], *plane[1:], after=[moved]
    )
    arrived = over_cores([column_rows, *crossed])
    keep, send = run(
        functools.partial(experts_body, len(arrived)),
        [((half, features), F32), ((half, features), BF16)],
        *arrived,
        w_gate,
        w_up,
        w_down,
        scratch=[pltpu.VMEM((all_rows, features), BF16)],
    )
    outs = run(
        functools.partial(add_student_body, size_x, 1),
        [((quarter, features), F32)]
        + [((quarter // 2, features), BF16)] * (2 * (size_x - 1))
        + split_rows,
        me,
        moved,
        moved_head,
        keep,
        swap(send, 1),
        *stud_parts,
        scalars=1,
        aliases={5 + i: 2 * size_x - 1 + i for i in range(size_x)},
    )
    keep, *sends = outs[: 2 * size_x - 1]
    stud_keep, *stud_sends = outs[2 * size_x - 1 :]
    far, near_rows = along(sends[::2]), along(sends[1::2])
    far = run(
        functools.partial(add_half_body, size_x - 1, True),
        [((tok_dev, features), BF16)] * (size_z // 2),
        keep,
        *far,
    )
    *near_rows, keep = run(
        functools.partial(add_half_body, size_x - 1, False),
        [((tok_dev, features), BF16)] * (size_z // 2 - 1) + [((tok_dev, features), F32)],
        keep,
        *near_rows,
    )
    summed = from_z(keep, [*far, *near_rows])
    outs = run(
        functools.partial(
            hidden_body,
            [0] + [2 * size_x * kz for kz in range(size_z - 1, 0, -1)],
            slices,
            len(stud_sends),
        ),
        [((tok_dev, features), BF16)] * size_z + [(a.shape, BF16) for a in stud_sends],
        me,
        *summed,
        tokens,
        final_gain,
        ids,
        scores,
        *stud_sends,
        scalars=1,
    )
    final_norms, stud_sends = outs[:size_z], outs[size_z:]
    column_rows, *outs = run(
        functools.partial(join_both_body, places(turn), size_x),
        [((quarter, features), BF16), *split_dev],
        *along_z(final_norms, turn),
        stud_keep,
        *along(stud_sends),
    )
    student = from_z(*take(outs))
    plane = along_x(column_rows)
    if near:
        (teacher_head,) = run(
            fetch_body,
            [(teacher_head.shape, BF16)],
            teacher_head,
            scratch=[pltpu.SemaphoreType.DMA((1,))],
            far=1,
            cost=(0, 2 * teacher_head.size),
            after=[column_rows],
        )
    keep, *sends = run(
        functools.partial(teacher_body, len(plane)),
        split_rows,
        *plane,
        teacher_head,
        their_teacher,
        moved,
        moved_head,
        scratch=[pltpu.VMEM((half, features), BF16)],
    )
    teacher = from_z(*take(add_x(keep, along(sends), combine_split_body)))
    divergence, grad = run(
        functools.partial(leave_body, len(teacher) - 1),
        [((1, tok_dev), F32), ((tok_dev, width), F32)],
        *teacher,
        *student,
        near_out=False,
    )
    return divergence.reshape(tok_dev), grad


def solution(mesh):
    placed = (
        P(("groups", "expert")),
        P(),
        P(("groups", "expert")),
        P(("groups", "expert")),
        P("expert", None),
        P("expert", None),
        P("expert", None),
        P(),
        P(None, "expert"),
        P("expert"),
        P("groups", "expert"),
        P(None, "expert"),
    )
    return jax.shard_map(
        per_device,
        mesh=mesh,
        in_specs=placed,
        out_specs=(P(("groups", "expert")), P(("groups", "expert"))),
        check_vma=False,
    )
```

```python
import functools

import jax
import jax.numpy as jnp
from jax import lax
from jax.experimental import pallas as pl
from jax.experimental.pallas import tpu as pltpu
from jax.sharding import PartitionSpec as P

FF = 2048
EPSILON = 1e-06
F32 = jnp.float32
BF16 = jnp.bfloat16
BLOCK = 128


def radices(devices):
    bits = devices.bit_length() - 1
    x_bits = (bits - 1) // 3
    return 1 << (bits - 1 - x_bits), 1 << x_bits, 2


def dot(a, b):
    return jnp.dot(a, b, preferred_element_type=F32)


def dot_t(a, b):
    return lax.dot_general(a, b, (((1,), (1,)), ((), ())), preferred_element_type=F32)


def lanes(rows):
    return lax.broadcasted_iota(jnp.int32, (rows, BLOCK), 1)


def pack(columns):
    lane = lanes(columns[0].shape[0])
    block = jnp.zeros(lane.shape, F32)
    for j, column in enumerate(columns):
        block = jnp.where((lane % 32 == j) & (lane < 96), column, block)
    return block


def split(block):
    lane = lanes(block.shape[0])
    high = block.astype(BF16)
    rest = block - high.astype(F32)
    middle = rest.astype(BF16)
    low = (rest - middle.astype(F32)).astype(BF16).astype(F32)
    return jnp.where(lane < 32, high.astype(F32), jnp.where(lane < 64, middle.astype(F32), low)).astype(BF16)


def column(block, j, exact):
    lane = lanes(block.shape[0])
    keep = (lane == j) if exact else (lane % 32 == j)
    return jnp.sum(jnp.where(keep, block, 0.0), axis=1, keepdims=True)


def combine(parts, width):
    blocks = [(ref[:, width:].astype(F32), i == 0) for i, ref in enumerate(parts)]
    tops = [column(b, 0, own) for b, own in blocks]
    top = functools.reduce(jnp.maximum, tops)
    scales = [jnp.exp(t - top) for t in tops]
    totals = [sum(column(b, j, own) * s for (b, own), s in zip(blocks, scales)) for j in (1, 2)]
    values = sum(ref[:, :width].astype(F32) * s for ref, s in zip(parts, scales))
    return values, top, totals


def call(body, outs, *args, scratch=(), scalars=0, after=(), far=0, near=True, near_out=True, limit=12, cost=None, aliases=None):
    smem = pl.BlockSpec(memory_space=pltpu.SMEM)
    vmem = pl.BlockSpec(memory_space=pltpu.VMEM)
    hbm = pl.BlockSpec(memory_space=pltpu.HBM)
    unread = pl.BlockSpec(memory_space=pl.ANY)
    count = len(args)
    middle = count - scalars - far

    def run(*refs):
        body(*refs[:count], *refs[count + len(after) :])

    if near:
        kinds = [None] * scalars + [pltpu.VMEM] * middle + [pltpu.HBM] * far
        args = [a if k is None else pltpu.with_memory_space_constraint(a, k) for a, k in zip(args, kinds)]
    kind = pltpu.VMEM if near and near_out else jax.ShapeDtypeStruct
    return pl.pallas_call(
        run,
        out_shape=[kind(s, d) for s, d in outs],
        in_specs=[smem] * scalars + [vmem] * middle + [hbm] * far + [unread] * len(after),
        out_specs=[vmem] * len(outs),
        scratch_shapes=list(scratch),
        input_output_aliases=aliases or {},
        compiler_params=pltpu.CompilerParams(vmem_limit_bytes=(limit if near else 56) * 2**20),
        cost_estimate=cost and pl.CostEstimate(flops=cost[0], bytes_accessed=cost[1], transcendentals=0),
    )(*args, *after)


def fetch(sources, targets, semaphores):
    copies = [
        pltpu.make_async_copy(source, target, semaphores.at[i])
        for i, (source, target) in enumerate(zip(sources, targets))
    ]
    for copy in copies:
        copy.start()
    return copies


def fetch_body(*refs):
    *refs, semaphores = refs
    for copy in fetch(refs[: len(refs) // 2], refs[len(refs) // 2 :], semaphores):
        copy.wait()


def normed_rows(values, gain):
    return values * lax.rsqrt(jnp.mean(values * values, axis=-1, keepdims=True) + EPSILON) * gain[None, :]


def early_body(gain_far, tokens_far, map_far, logits_far, gain, tokens, entries, vocab_map, semaphores):
    count = logits_far.shape[0]
    copies = fetch(
        (map_far, logits_far, gain_far, tokens_far),
        (vocab_map, entries.at[:count], gain, tokens),
        semaphores,
    )
    copies[0].wait()
    places = vocab_map[...].astype(F32)[None, :]
    entries[count:, :] = jnp.broadcast_to(places, (16, places.shape[1])).astype(BF16)
    for copy in copies[1:]:
        copy.wait()


def paired(out):
    return [slice(at, at + 16) for at in range(0, out.shape[0], 16)]


def join_body(turns, *refs):
    *parts, out = refs
    parts = [parts[i] for i in turns]
    for rows, pair in zip(paired(out), zip(*[iter(parts)] * 2)):
        out[rows, :] = jnp.concatenate([p[...].astype(F32) for p in pair]).astype(BF16)


def join_normed_body(turns, gain, *refs):
    *parts, out = refs
    parts = [parts[i] for i in turns]
    for rows, pair in zip(paired(out), zip(*[iter(parts)] * 2)):
        joined = jnp.concatenate([p[...].astype(F32) for p in pair])
        out[rows, :] = normed_rows(joined, gain[...]).astype(BF16)


def experts_body(parts, *refs):
    inputs, (w_gate, w_up, w_down, keep, send, rows_ref) = refs[:parts], refs[parts:]
    count = inputs[0].shape[0]
    features = w_gate.shape[1]
    for i, ref in enumerate(inputs):
        rows_ref[i * count : (i + 1) * count, :] = ref[:, : rows_ref.shape[1]]

    def block(start, size):
        rows = rows_ref[pl.ds(start, size), :]
        gate = dot(rows, w_gate[0])
        up = dot(rows, w_up[0])
        return (gate / (1.0 + jnp.exp(-gate)) * up).astype(BF16)

    half = parts * count // 2
    if half < BLOCK:
        activated = block(0, 2 * half)
        step = 512
        for at in range(0, features, step):
            out = dot(activated, w_down[0, :, at : at + step])
            keep[:, at : at + step] = out[:half]
            send[:, at : at + step] = out[half:].astype(BF16)
    else:
        for h, target in enumerate((keep, send)):

            @pl.loop(0, half // BLOCK)
            def _(i):
                start = pl.multiple_of(i * BLOCK, BLOCK)
                activated = block(h * half + start, BLOCK)
                out = dot(activated, w_down[0])
                target[pl.ds(start, BLOCK), :] = out.astype(target.dtype)


def add_split_body(received, *refs):
    parts, (keep, *sends) = refs[: received + 1], refs[received + 1 :]
    total = sum((ref[...].astype(F32) for ref in parts[1:]), parts[0][...])
    rows = keep.shape[0]
    keep[...] = total[:rows]
    for i, send in enumerate(sends):
        at = (len(sends) - i) * rows
        send[...] = total[at : at + rows].astype(BF16)


def hidden_body(offsets, slices, passing, me, *refs):
    parts, (tokens, gain, ids, scores, *refs) = refs[: len(offsets)], refs[len(offsets) :]
    passed, outs = refs[:passing], refs[passing:]
    rows = tokens.shape[0]
    diagonal = lax.broadcasted_iota(jnp.int32, (rows, rows), 0) == lax.broadcasted_iota(
        jnp.int32, (rows, rows), 1
    )

    def down(values):
        return jnp.sum(jnp.where(diagonal, values, 0.0), axis=1, keepdims=True)

    chosen = [down(ids[k : k + 1, :].astype(F32)) for k in range(ids.shape[0])]
    score = [down(scores[k : k + 1, :]) for k in range(ids.shape[0])]
    whole = sum(score)
    total = tokens[...].astype(F32)
    for ref, offset in zip(parts, offsets):
        expert = ((me[0] ^ offset) // slices).astype(F32)
        weight = sum(jnp.where(c == expert, v, 0.0) for c, v in zip(chosen, score)) / whole
        total = total + ref[...].astype(F32) * weight
    normed = normed_rows(total, gain[...]).astype(BF16)
    for out in outs[: len(outs) - passing]:
        out[...] = normed
    for source, target in zip(passed, outs[len(outs) - passing :]):
        target[...] = source[...]


def student_body(devices, order, prefetched, me, ours, theirs, their_head, head_far, *refs):
    sources, (moved, moved_head, *refs) = refs[:prefetched], refs[prefetched:]
    parts = refs[: len(refs) - prefetched - 3]
    refs = refs[len(parts) :]
    targets, (head, scratch, semaphores) = refs[:prefetched], refs[prefetched:]
    copies = fetch((head_far, *sources), (head, *targets), semaphores)
    copies[0].wait()
    count = scratch.shape[0]
    entries = head.shape[1]
    tok_dev = count // devices
    for i, (rows, weights) in enumerate(((ours, head), (theirs, their_head))):
        cols = slice(i * entries, (i + 1) * entries)
        index = lax.broadcasted_iota(jnp.int32, (entries, entries), 0).astype(F32)
        place = index == rows[count:, :].astype(F32)[:1, :]
        place = jnp.where(place, 1.0, 0.0).astype(BF16)
        scratch[:, cols] = dot_t(rows[:count, :], place)
        moved_head[:, cols] = dot_t(weights[...], place).astype(BF16)
    for slot, offset in enumerate(order):
        source = pl.multiple_of((me[0] ^ offset) * tok_dev, tok_dev)
        moved[slot * tok_dev : (slot + 1) * tok_dev, :] = scratch[pl.ds(source, tok_dev), :]

    width = moved_head.shape[0]
    student_part(moved, moved_head, parts, 0, late(width))

    @pl.when(me[0] % 2 == 1)
    def _():
        student_part(moved, moved_head, parts, late(width), width)

    for copy in copies[1:]:
        copy.wait()


def late(width):
    return width - width // 2 // BLOCK * BLOCK


def student_part(moved, moved_head, targets, start, stop):
    step = min(moved.shape[0], BLOCK)
    for at in range(0, moved.shape[0], step):
        student = moved[at : at + step, :]
        top = jnp.max(student, axis=1, keepdims=True)
        exps = jnp.exp(student - top)
        total = jnp.sum(exps, axis=1, keepdims=True)
        emit(at, step, exps, moved_head, [top, total, jnp.zeros_like(top)], targets, start, stop)


def add_student_body(parts, received, me, moved, moved_head, *refs):
    summands, refs = refs[: received + 1], refs[received + 1 + parts :]
    add_split_body(received, *summands, *refs[:-parts])

    @pl.when(me[0] % 2 == 0)
    def _():
        width = moved_head.shape[0]
        student_part(moved, moved_head, refs[-parts:], late(width), width)


def emit(at, step, exps, head, columns, targets, start, stop):
    stats = pack(columns)
    values = dot_t(exps.astype(BF16), head[start:stop, :])
    width = head.shape[0]
    for i, target in enumerate(targets):
        rows = target.shape[0]
        low, high = max(at, i * rows), min(at + step, (i + 1) * rows)
        if low < high:
            inner, outer = slice(low - at, high - at), slice(low - i * rows, high - i * rows)
            target[outer, start:stop] = values[inner].astype(target.dtype)
            target[outer, width:] = stats[inner] if i == 0 else split(stats[inner])


def teacher_body(parts, *refs):
    inputs, (head, their_head, moved, moved_head, *targets, rows_ref) = refs[:parts], refs[parts:]
    count = inputs[0].shape[0]
    for i, ref in enumerate(inputs):
        rows_ref[i * count : (i + 1) * count, :] = ref[...]
    step = min(parts * count, BLOCK)
    for at in range(0, parts * count, step):
        rows = rows_ref[at : at + step, :]
        teacher = jnp.concatenate([dot(rows, head[...]), dot(rows, their_head[...])], axis=1)
        student = moved[at : at + step, :]
        top = jnp.max(teacher, axis=1, keepdims=True)
        exps = jnp.exp(teacher - top)
        total = jnp.sum(exps, axis=1, keepdims=True)
        cross = jnp.sum(exps * (teacher - student), axis=1, keepdims=True)
        emit(at, step, exps, moved_head, [top, total, cross], targets, 0, moved_head.shape[0])


def combine_split_body(received, *refs):
    parts, (keep, *sends) = refs[: received + 1], refs[received + 1 :]
    width = keep.shape[1] - BLOCK
    values, top, totals = combine(parts, width)
    stats = pack([top, *totals])
    coded = split(stats)
    rows = keep.shape[0]
    keep[:, :width] = values[:rows]
    keep[:, width:] = stats[:rows]
    for i, send in enumerate(sends):
        at = (len(sends) - i) * rows
        inner = slice(at, at + rows)
        send[:, :width] = values[inner].astype(BF16)
        send[:, width:] = coded[inner]


def pass_body(*refs):
    for source, target in zip(refs[: len(refs) // 2], refs[len(refs) // 2 :]):
        target[...] = source[...]


def join_both_body(turns, size_x, *refs):
    parts, refs = refs[: len(turns)], refs[len(turns) :]
    student, (out, *outs) = refs[:size_x], refs[size_x:]
    join_body(turns, *parts, out)
    combine_split_body(size_x - 1, *student, *outs)


def leave_body(received, *refs):
    teacher, refs = refs[: received + 1], refs[received + 1 :]
    student, (divergence, grad) = refs[: received + 1], refs[received + 1 :]
    width = grad.shape[1]
    teach_values, teach_max, (teach_sum, cross_sum) = combine(teacher, width)
    stud_values, stud_max, (stud_sum, _) = combine(student, width)
    grad[...] = stud_values / stud_sum - teach_values / teach_sum
    value = cross_sum / teach_sum - teach_max - jnp.log(teach_sum) + stud_max + jnp.log(stud_sum)
    rows = grad.shape[0]
    diagonal = lax.broadcasted_iota(jnp.int32, (rows, rows), 0) == lax.broadcasted_iota(
        jnp.int32, (rows, rows), 1
    )
    divergence[...] = jnp.sum(jnp.where(diagonal, value, 0.0), axis=0, keepdims=True)


def take(outs):
    return outs[0], outs[1:]


def per_device(
    tokens,
    moe_gain,
    expert_ids,
    gate_scores,
    w_gate,
    w_up,
    w_down,
    final_gain,
    teacher_head,
    vocab_map,
    student_logits,
    student_head,
):
    devices = lax.axis_size("expert")
    size_z, size_x, _ = radices(devices)
    me = lax.axis_index("expert").astype(jnp.int32).reshape(1)
    tok_dev, features = tokens.shape
    slices = FF // w_gate.shape[2]
    width = student_head.shape[0]
    all_rows = devices * tok_dev
    half, quarter = all_rows // 2, all_rows // (2 * size_x)
    entries = student_head.shape[1]
    order = [kz * 2 * size_x + kx * 2 for kx in range(size_x) for kz in range(size_z)]
    near = all_rows <= BLOCK
    run = functools.partial(call, near=near)

    def swap(values, offset):
        return lax.ppermute(values, "expert", [(i, i ^ offset) for i in range(devices)])

    def places(turn):
        return [list(turn).index(kz) if kz else len(turn) for kz in range(size_z)]

    def along_z(rows, turn):
        return [*(swap(rows[kz], kz * 2 * size_x) for kz in turn), rows[0]]

    def along_x(column):
        return [column] + [swap(column, kx * 2) for kx in range(1, size_x)]

    def over_cores(plane):
        return plane + [swap(part, 1) for part in plane]

    def add_x(keep, sends, body, after=()):
        outs = [((tok_dev, keep.shape[1]), d) for d in [F32] + [BF16] * (size_z - 1)]
        return run(functools.partial(body, size_x - 1), outs, keep, *sends, after=after)

    def along(sends):
        return [swap(s, 2 * (size_x - 1 - i)) for i, s in enumerate(sends)]

    def from_z(keep, sends):
        return [keep] + [swap(s, 2 * size_x * (size_z - 1 - i)) for i, s in enumerate(sends)]

    turn = list(range(size_z - 1, 0, -1))
    first_turn = [size_z - 1, *range(1, size_z - 1)]
    parts = along_z([tokens] * size_z, first_turn)
    moe_gain, tokens, ours = run(
        early_body,
        [(moe_gain.shape, F32), (tokens.shape, BF16), ((all_rows + 16, entries), BF16)],
        moe_gain,
        tokens,
        vocab_map,
        student_logits,
        scratch=[pltpu.VMEM((entries,), jnp.int32), pltpu.SemaphoreType.DMA((4,))],
        far=4,
        after=parts[:1],
    )
    parts[-1] = tokens
    theirs = swap(ours, 1)
    (column_rows,) = run(
        functools.partial(join_normed_body, places(first_turn)),
        [((quarter, features), BF16)],
        moe_gain,
        *parts,

    )
    plane = along_x(column_rows)
    their_head = swap(student_head, 1)
    their_teacher = swap(teacher_head, 1)
    prefetched = [w_gate, w_up, w_down, teacher_head, final_gain, expert_ids.T, gate_scores.T]
    fetched = prefetched if near else []
    split_rows = [((quarter, width + BLOCK), d) for d in [F32] + [BF16] * (size_x - 1)]
    split_dev = [((tok_dev, width + BLOCK), d) for d in [F32] + [BF16] * (size_z - 1)]
    outs = run(
        functools.partial(student_body, devices, order, len(fetched)),
        [
            ((half, 2 * entries), F32),
            ((width, 2 * entries), BF16),
            *split_rows,
            *[(a.shape, a.dtype) for a in fetched],
        ],
        me,
        ours,
        theirs,
        their_head,
        student_head,
        *fetched,
        scratch=[
            pltpu.VMEM((width, entries), BF16),
            pltpu.VMEM((all_rows, 2 * entries), F32),
            pltpu.SemaphoreType.DMA((1 + len(fetched),)),
        ],
        scalars=1,
        far=1 + len(fetched),
        cost=(4 * entries * width * (half + entries), 2 * sum(a.size for a in prefetched)),
        after=[column_rows],
    )
    moved, moved_head, *stud_parts = outs[: 2 + size_x]
    w_gate, w_up, w_down, teacher_head, final_gain, ids, scores = (
        outs[2 + size_x :] if near else prefetched
    )
    crossed = run(
        pass_body, [(p.shape, p.dtype) for p in plane[1:]], *plane[1:], after=[moved]
    )
    arrived = over_cores([column_rows, *crossed])
    keep, send = run(
        functools.partial(experts_body, len(arrived)),
        [((half, features), F32), ((half, features), BF16)],
        *arrived,
        w_gate,
        w_up,
        w_down,
        scratch=[pltpu.VMEM((all_rows, features), BF16)],
    )
    outs = run(
        functools.partial(add_student_body, size_x, 1),
        [((quarter, features), d) for d in [F32] + [BF16] * (size_x - 1)] + split_rows,
        me,
        moved,
        moved_head,
        keep,
        swap(send, 1),
        *stud_parts,
        scalars=1,
        aliases={5 + i: size_x + i for i in range(size_x)},
    )
    keep, *sends = outs[:size_x]
    stud_keep, *stud_sends = outs[size_x:]
    summed = from_z(*take(add_x(keep, along(sends), add_split_body)))
    outs = run(
        functools.partial(
            hidden_body,
            [0] + [2 * size_x * kz for kz in range(size_z - 1, 0, -1)],
            slices,
            len(stud_sends),
        ),
        [((tok_dev, features), BF16)] * size_z + [(a.shape, BF16) for a in stud_sends],
        me,
        *summed,
        tokens,
        final_gain,
        ids,
        scores,
        *stud_sends,
        scalars=1,
    )
    final_norms, stud_sends = outs[:size_z], outs[size_z:]
    column_rows, *outs = run(
        functools.partial(join_both_body, places(turn), size_x),
        [((quarter, features), BF16), *split_dev],
        *along_z(final_norms, turn),
        stud_keep,
        *along(stud_sends),
    )
    student = from_z(*take(outs))
    plane = along_x(column_rows)
    keep, *sends = run(
        functools.partial(teacher_body, len(plane)),
        split_rows,
        *plane,
        teacher_head,
        their_teacher,
        moved,
        moved_head,
        scratch=[pltpu.VMEM((half, features), BF16)],
    )
    teacher = from_z(*take(add_x(keep, along(sends), combine_split_body)))
    divergence, grad = run(
        functools.partial(leave_body, len(teacher) - 1),
        [((1, tok_dev), F32), ((tok_dev, width), F32)],
        *teacher,
        *student,
        near_out=False,
    )
    return divergence.reshape(tok_dev), grad


def solution(mesh):
    placed = (
        P(("groups", "expert")),
        P(),
        P(("groups", "expert")),
        P(("groups", "expert")),
        P("expert", None),
        P("expert", None),
        P("expert", None),
        P(),
        P(None, "expert"),
        P("expert"),
        P("groups", "expert"),
        P(None, "expert"),
    )
    return jax.shard_map(
        per_device,
        mesh=mesh,
        in_specs=placed,
        out_specs=(P(("groups", "expert")), P(("groups", "expert"))),
        check_vma=False,
    )
```
